256 devices in a mesh: py: 16 (over z, core), pz: 16 (over x, y).
Axes of the slice: x: 4, y: 4, z: 8, core: 2. Of those that a mesh axis runs over, the one named last changes fastest.
Arguments:
- velocity: float32 [192, 384, 1536], P('pz', 'py'), may hold values from -4 to 4
- wind_profile: float32 [192], P('pz'), may hold values from 0.5 to 1.5
- thrust_coef: float32 [100], replicated, may hold values from 0.5 to 2
- turbine_bricks: int32 [100, 4], replicated, may hold values from 0 to 383, as said below
- turbine_offset: int32 [100, 3], replicated, may hold values from 6 to 95, as said below
Outputs:
- tendency: float32 [192, 384, 1536], P('pz', 'py')
- rotor_speed: float32 [100], replicated
The draws below stay inside these ranges and needn't reach their ends.
Inputs may be any that keep to these rules, and one draw needn't show every extreme that they name: `turbine_bricks`: row t lists the bricks (0, j, b), (0, j + 1, b), (1, j, b), (1, j + 1, b) in this order, as (pz row, py column, x block) coded as in the reference program, with j + 1 below the number of py devices and b below both 1536 / 128 and the number of py devices; no two turbines have the same (j, b). `turbine_offset`: oz lies in [h / 2, 3 h / 2) with h = 192 / 16, oy in [w / 2, 3 w / 2) with w = 384 / 16, ox in [32, 96).
All inputs are finite; a program needn't handle non-finite values.
Results may differ from the reference program's by a relative error of at most 0.000064.
Values sent between devices are 32-bit elements; how exact they have to be, the bound alone decides.
No kernel may reach another device: no remote copies, remote signals or barrier semaphores. Data moves between devices by JAX's collectives and lax.ppermute only.
A program may use at most 192 MiB of HBM per device.

```python
import math
import jax
import jax.numpy as jnp
from jax import lax

NX = 1536
NY = 384
NZ = 192
BX = 128
TURB = 100
N_PY = 16
N_PZ = 16


def draw_turbine_bricks(key, part):
    key = jax.random.fold_in(key, 1)
    blocks_x = NX // BX
    usable = min(blocks_x, N_PY)
    columns = N_PY - 1
    ordering = jax.random.permutation(key, usable * columns)
    chosen = ordering[:TURB].astype(jnp.int32)
    x_block = chosen % usable
    left_column = chosen // usable
    listed = []
    for level in range(2):
        for step_y in range(2):
            listed.append((level * N_PY + left_column + step_y) * blocks_x + x_block)
    return jnp.stack(listed, axis=1).astype(jnp.int32)


def draw_turbine_offset(key, part):
    key = jax.random.fold_in(key, 2)
    depth_z = NZ // N_PZ
    span_y = NY // N_PY
    key_z, key_y, key_x = jax.random.split(key, 3)
    offset_z = jax.random.randint(key_z, (TURB,), depth_z // 2, depth_z + depth_z // 2)
    offset_y = jax.random.randint(key_y, (TURB,), span_y // 2, span_y + span_y // 2)
    offset_x = jax.random.randint(key_x, (TURB,), BX // 4, 3 * BX // 4)
    offset_z = offset_z.at[0].set(depth_z // 2).at[1].set(depth_z + depth_z // 2 - 1)
    offset_y = offset_y.at[0].set(span_y // 2).at[1].set(span_y + span_y // 2 - 1)
    offset_x = offset_x.at[0].set(BX // 4).at[1].set(3 * BX // 4 - 1)
    return jnp.stack([offset_z, offset_y, offset_x], axis=1).astype(jnp.int32)


def block_levels(rng, extent, cuts, least, top_value):
    level = 1.0
    for dim, parts in cuts:
        steps = jax.random.uniform(jax.random.fold_in(jax.random.fold_in(rng, 6), dim), (parts,), jnp.float32, least / len(cuts), top_value / len(cuts))
        level = level * jnp.repeat(jnp.exp(steps), extent[dim] // parts).reshape((-1,) + (1,) * (len(extent) - 1 - dim))
    return level


def noise(key, dims, spread, most, shards=(), held_as=jnp.bfloat16):
    factor_of = block_levels(key, dims, shards, -0.22, 0.18) if shards else 1.0
    values = jax.random.normal(key, dims, jnp.float32) * spread * factor_of
    return jnp.minimum(jnp.maximum(values, -most), most).astype(held_as)


def setup_inputs(seed: int = 0) -> dict:
    keys = jax.random.split(jax.random.key(seed), 6)
    velocity = noise(keys[0], (NZ, NY, NX), 0.3, 4.0, ((0, 16), (1, 16)), jnp.float32)
    wind_profile = jnp.clip(jnp.exp(math.log(1.5) - 1.0986123 * jax.random.uniform(keys[1], (NZ,), jnp.float32) ** block_levels(keys[1], (NZ,), ((0, 16),), -0.2, 0.2)), 0.5, 1.5)
    thrust_coef = jnp.clip(jnp.exp(jax.random.uniform(keys[2], (TURB,), jnp.float32, math.log(0.5), math.log(2.0))), 0.5, 2.0)
    turbine_bricks = draw_turbine_bricks(jax.random.fold_in(keys[5], 71), 0)
    turbine_offset = draw_turbine_offset(jax.random.fold_in(keys[5], 71), 0)
    return {"velocity": velocity, "wind_profile": wind_profile, "thrust_coef": thrust_coef, "turbine_bricks": turbine_bricks, "turbine_offset": turbine_offset}


VISCOSITY = 0.2
CROSS_WIND = 0.4
DISK_DEPTH = 1.5
DISK_EDGE = 1.0
RADIUS_SHARE = 0.6


def spectral(values, dimension, second_weight, first_weight):
    length = values.shape[dimension]
    waves = (2.0 * math.pi * jnp.fft.rfftfreq(length)).astype(values.dtype)
    nyquist = jnp.arange(waves.shape[0]) == length // 2
    slopes = jnp.where(nyquist, 0.0, waves).astype(values.dtype)
    layout = [1, 1, 1]
    layout[dimension] = -1
    factor = (-second_weight * waves * waves).reshape(layout) + 1j * (first_weight * slopes).reshape(layout)
    spectrum = jnp.fft.rfft(values, axis=dimension)
    return jnp.fft.irfft(spectrum * factor, n=length, axis=dimension).astype(values.dtype)


def disk_weights(rel_z, rel_y, rel_x, radius):
    axial = jnp.exp(-0.5 * (rel_x / DISK_DEPTH) ** 2)
    radial = jax.nn.sigmoid((radius * radius - rel_y * rel_y - rel_z * rel_z) / (2.0 * radius * DISK_EDGE))
    return axial * radial


def reference(velocity, wind_profile, thrust_coef, turbine_bricks, turbine_offset):
    depth_z = NZ // N_PZ
    span_y = NY // N_PY
    blocks_x = NX // BX
    radius = RADIUS_SHARE * depth_z
    base_brick = turbine_bricks[:, 0]
    left_column = (base_brick // blocks_x) % N_PY
    x_block = base_brick % blocks_x
    anchor_y = (left_column * span_y).astype(jnp.int32)
    anchor_x = (x_block * BX).astype(jnp.int32)
    offsets = turbine_offset.astype(jnp.float32)
    height = jnp.arange(2 * depth_z, dtype=jnp.int32).astype(jnp.float32)
    across = jnp.arange(2 * span_y, dtype=jnp.int32).astype(jnp.float32)
    along_x = jnp.arange(BX, dtype=jnp.int32).astype(jnp.float32)
    zero_index = jnp.zeros((), jnp.int32)
    shape_window = (2 * depth_z, 2 * span_y, BX)
    winds_low = wind_profile[:2 * depth_z][:, None, None]

    def weights_of(turbine):
        rel_z = (height - offsets[turbine, 0])[:, None, None]
        rel_y = (across - offsets[turbine, 1])[None, :, None]
        rel_x = (along_x - offsets[turbine, 2])[None, None, :]
        return disk_weights(rel_z, rel_y, rel_x, radius)

    def measure(turbine):
        window_field = lax.dynamic_slice(velocity, (zero_index, anchor_y[turbine], anchor_x[turbine]), shape_window)
        weights = weights_of(turbine)
        return jnp.sum(weights * (winds_low + window_field)), jnp.sum(weights)

    turbines = jnp.arange(TURB, dtype=jnp.int32)
    numerator, denominator = lax.map(measure, turbines)
    rotor_speed = numerator / denominator
    thrust = -0.5 * thrust_coef * rotor_speed * jnp.abs(rotor_speed)

    def deposit(force, turbine):
        start_at = (zero_index, anchor_y[turbine], anchor_x[turbine])
        window_force = lax.dynamic_slice(force, start_at, shape_window) + thrust[turbine] * weights_of(turbine)
        return lax.dynamic_update_slice(force, window_force, start_at), None

    force, unused_out = lax.scan(deposit, jnp.zeros(velocity.shape, jnp.float32), turbines)
    profile = wind_profile[:, None, None]
    tendency = spectral(velocity, 2, VISCOSITY, 0.0) - profile * spectral(velocity, 2, 0.0, 1.0)
    tendency = tendency + spectral(velocity, 1, VISCOSITY, -CROSS_WIND)
    tendency = tendency + spectral(velocity, 0, VISCOSITY, 0.0) + force
    return tendency, rotor_speed
```

```python
import math

import jax
import jax.numpy as jnp
import ml_dtypes
import numpy as np
from jax import lax
from jax.experimental import pallas as pl
from jax.experimental.pallas import tpu as pltpu
from jax.sharding import PartitionSpec as P

NX, NY, NZ, BX = 1536, 384, 192, 128
TURB = 100
N = 16
DZ, DY, XB = NZ // N, NY // N, NX // BX
HALF = NX // 2
VISCOSITY = 0.2
CROSS_WIND = 0.4
DISK_DEPTH = 1.5
RADIUS = 0.6 * DZ
F32, BF16 = jnp.float32, jnp.bfloat16
VM = pl.BlockSpec(memory_space=pltpu.VMEM)
SM = pl.BlockSpec(memory_space=pltpu.SMEM)
ROUTES = (("x", "y", (0, 1, 2, 3, 4)), ("y", "x", (5, 6, 7, 8)))


def params(mib=40):
    return pltpu.CompilerParams(vmem_limit_bytes=mib * 1024 * 1024)


def kernels_of(length):
    m = np.arange(length)
    m = np.where(m > length // 2, m - length, m).astype(np.float64)
    parity = np.where(m % 2 == 0, 1.0, -1.0)
    angle = math.pi / length * m
    sine = np.where(m == 0, 1.0, np.sin(angle))
    first = np.where(m == 0, 0.0, math.pi / length * parity * np.cos(angle) / sine)
    second = np.where(
        m == 0,
        -math.pi**2 / 3.0 - 2.0 * math.pi**2 / (3.0 * length * length),
        -(2.0 * math.pi**2 / (length * length)) * parity / (sine * sine),
    )
    return first, second


def split(table):
    high = table.astype(np.float32).astype(ml_dtypes.bfloat16)
    low = (table - high.astype(np.float64)).astype(np.float32).astype(ml_dtypes.bfloat16)
    return high, low


def x_tables():
    first, second = kernels_of(NX)
    source, target = np.arange(HALF)[:, None], np.arange(HALF)[None, :]
    near, far = (target - source) % NX, (target - source + HALF) % NX
    mats = []
    for sign in (1.0, -1.0):
        for table in (VISCOSITY * second, first):
            mats.extend(split(0.5 * (table[near] + sign * table[far])))
    stacked = np.stack(mats)
    return np.ascontiguousarray(
        stacked.reshape(8, HALF, 3, 256).transpose(2, 0, 1, 3)
    )


def y_matrix():
    first, second = kernels_of(NY)
    i = np.arange(NY)
    return split((VISCOSITY * second - CROSS_WIND * first)[(i[:, None] - i[None, :]) % NY])


def z_matrix():
    _, second = kernels_of(NZ)
    row = np.arange(N * 2 * DZ)
    block, inner = row // (2 * DZ), row % (2 * DZ)
    half, height = inner // DZ, block * DZ + inner % DZ
    table = VISCOSITY * second[(height[:, None] - height[None, :]) % NZ]
    return split(np.where(half[:, None] == half[None, :], table, 0.0))


def halves(value):
    high = value.astype(BF16)
    return high, (value - high.astype(F32)).astype(BF16)


def dot(a, b):
    return jnp.dot(a, b, preferred_element_type=F32)


def x_kernel(wind_ref, v_ref, table_ref, out_ref, lhs_ref):
    step = pl.program_id(0)
    rows = DZ * DY

    @pl.when(step == 0)
    def _():
        low_x = v_ref[:, :, :HALF].reshape(rows, HALF)
        high_x = v_ref[:, :, HALF:].reshape(rows, HALF)
        for part, value in enumerate((low_x + high_x, low_x - high_x)):
            high, low = halves(value)
            lhs_ref[part, :rows] = high
            lhs_ref[part, rows:] = low

    terms = []
    for part in range(2):
        lhs = lhs_ref[part]
        got = []
        for which in range(2):
            both = dot(lhs, table_ref[0, 4 * part + 2 * which])
            extra = dot(lhs[:rows], table_ref[0, 4 * part + 2 * which + 1])
            got.append((both[:rows] + both[rows:] + extra).reshape(DZ, DY, 256))
        terms.append(got)
    here = pl.ds(pl.multiple_of(step * 256, 256), 256)
    there = pl.ds(pl.multiple_of(HALF + step * 256, 256), 256)
    for z in range(DZ):
        even = terms[0][0][z] - wind_ref[z] * terms[0][1][z]
        odd = terms[1][0][z] - wind_ref[z] * terms[1][1][z]
        out_ref[z, :, here] = even + odd
        out_ref[z, :, there] = even - odd


def along_x(velocity, wind):
    tables = jnp.asarray(x_tables())
    return pl.pallas_call(
        x_kernel,
        grid=(3,),
        in_specs=[
            SM,
            pl.BlockSpec((DZ, DY, NX), lambda i: (0, 0, 0)),
            pl.BlockSpec((1, 8, HALF, 256), lambda i: (i, 0, 0, 0)),
        ],
        out_specs=pl.BlockSpec((DZ, DY, NX), lambda i: (0, 0, 0)),
        out_shape=jax.ShapeDtypeStruct((DZ, DY, NX), F32),
        scratch_shapes=[pltpu.VMEM((2, 2 * DZ * DY, HALF), BF16)],
        compiler_params=params(),
        cost_estimate=pl.CostEstimate(
            flops=2 * 288 * 768 * 768 * 12, bytes_accessed=13 * 2**20, transcendentals=0
        ),
        name="x_derivative",
    )(wind, velocity, tables)


def y_pack_kernel(v_ref, out_ref):
    for local in range(36):
        d, j = local // 9, local % 9
        z, xb = local // XB, local % XB
        for yt in range(3):
            out_ref[d, yt * 9 + j] = v_ref[z, yt * 8 : yt * 8 + 8, xb * BX : xb * BX + BX]


def y_pack(velocity):
    return pl.pallas_call(
        y_pack_kernel,
        grid=(4,),
        in_specs=[pl.BlockSpec((3, DY, NX), lambda i: (i, 0, 0))],
        out_specs=pl.BlockSpec((4, 27, 8, BX), lambda i: (i, 0, 0, 0)),
        out_shape=jax.ShapeDtypeStruct((N, 27, 8, BX), F32),
        compiler_params=params(16),
        name="y_pack",
    )(velocity)


def line_product(high_ref, low_ref, read, write):
    for group in range(3):
        tiles = [read(group * 3 + k) for k in range(3)]
        high, low = halves(jnp.concatenate(tiles, axis=1))
        got = dot(high_ref[...], high) + dot(low_ref[...], high) + dot(high_ref[...], low)
        for k in range(3):
            write(group * 3 + k, got[:, k * BX : k * BX + BX])


def y_kernel(high_ref, low_ref, in_ref, sums_ref, out_ref):
    def read(j):
        return jnp.stack([in_ref[:, yt * 9 + j] for yt in range(3)], axis=1).reshape(NY, BX)

    def write(j, value):
        value = value.reshape(N, 3, 8, BX)
        for yt in range(3):
            out_ref[:, yt * 9 + j] = value[:, yt]

    line_product(high_ref, low_ref, read, write)
    for d in range(N):
        out_ref[d, 27] = sums_ref[...]


def y_lines(received, sums):
    high, low = y_matrix()
    return pl.pallas_call(
        y_kernel,
        in_specs=[VM] * 4,
        out_specs=VM,
        out_shape=jax.ShapeDtypeStruct((N, 28, 8, BX), F32),
        compiler_params=params(),
        name="y_lines",
    )(jnp.asarray(high), jnp.asarray(low), received, sums)


def device_at(route, place_first, place_second):
    return place_first * 4 + place_second if route[0] == "x" else place_second * 4 + place_first


def places(route, where_ref):
    x, y = where_ref[1], where_ref[2]
    return (x, y) if route[0] == "x" else (y, x)


def tiles_of(route):
    return 3 * len(route[2])


def columns_of(device, j, h):
    y = (device // 2) * 3 + j // 3
    xb = ((device % 2) * 2 + h) * 3 + j % 3
    return y, xb


def z_pack_kernel(where_ref, in_ref, sums_ref, *refs):
    out_refs, v_ref = refs[:8], refs[8]
    for xb in range(XB):
        v_ref[xb] = in_ref[:, xb * BX : xb * BX + BX]
    for r, route in enumerate(ROUTES):
        first, second = places(route, where_ref)
        width = len(route[2])
        for k1 in range(4):
            out = out_refs[r * 4 + k1]
            out[4 * 3 * width] = sums_ref[...]
            for k2 in range(4):
                device = device_at(route, (first + k1) % 4, (second + k2) % 4)
                for n, j in enumerate(route[2]):
                    y, low_cols = columns_of(device, j, 0)
                    y, high_cols = columns_of(device, j, 1)
                    base = k2 * 3 * width + n
                    out[base] = v_ref[low_cols, pl.ds(y, 8, stride=DY), :]
                    out[base + width, 0:4] = v_ref[low_cols, pl.ds(y + 8 * DY, 4, stride=DY), :]
                    out[base + width, 4:8] = v_ref[high_cols, pl.ds(y, 4, stride=DY), :]
                    out[base + 2 * width] = v_ref[high_cols, pl.ds(y + 4 * DY, 8, stride=DY), :]


def z_pack(where, velocity, sums):
    shapes = []
    for route in ROUTES:
        shapes += [jax.ShapeDtypeStruct((4 * tiles_of(route) + 1, 8, BX), F32)] * 4
    return pl.pallas_call(
        z_pack_kernel,
        in_specs=[SM, VM, VM],
        out_specs=[VM] * 8,
        out_shape=shapes,
        scratch_shapes=[pltpu.VMEM((XB, DZ * DY, BX), F32)],
        compiler_params=params(),
        name="z_pack",
    )(where, velocity.reshape(DZ * DY, NX), sums)


def regroup(arrays, tiles, with_sums):
    def kernel(*refs):
        for i in range(4):
            for k in range(4):
                refs[4 + i][k * tiles : (k + 1) * tiles] = refs[k][i * tiles : (i + 1) * tiles]
            if with_sums:
                last = 4 * tiles
                refs[4 + i][last] = (refs[0][last] + refs[1][last]) + (refs[2][last] + refs[3][last])

    shape = jax.ShapeDtypeStruct((4 * tiles + (1 if with_sums else 0), 8, BX), F32)
    return pl.pallas_call(
        kernel,
        in_specs=[VM] * 4,
        out_specs=[VM] * 4,
        out_shape=[shape] * 4,
        compiler_params=params(16),
        name="regroup",
    )(*arrays)


def shift(value, axis, by):
    moves = []
    for i in range(N):
        x, y = i // 4, i % 4
        moves.append((i, ((x + by) % 4) * 4 + y if axis == "x" else x * 4 + (y + by) % 4))
    return lax.ppermute(value, "pz", moves)


def send_stage(arrays, axis, sign):
    return [arrays[0]] + [shift(arrays[k], axis, sign * k) for k in range(1, 4)]


def z_kernel(where_ref, high_ref, low_ref, *refs):
    ins, outs, sums_ref, lines_ref = refs[:8], refs[8:16], refs[16], refs[17]
    total = None
    for r, route in enumerate(ROUTES):
        first, second = places(route, where_ref)
        tiles, width = tiles_of(route), len(route[2])
        for k2 in range(4):
            got = ins[r * 4 + k2]
            if r == 0:
                total = got[4 * tiles] if total is None else total + got[4 * tiles]
            for k1 in range(4):
                source = device_at(route, (first - k1) % 4, (second - k2) % 4)
                for rt in range(3):
                    at = k1 * tiles + rt * width
                    lines_ref[source, rt * 9 + route[2][0] : rt * 9 + route[2][0] + width] = got[at : at + width]
    sums_ref[...] = total

    def read(j):
        return jnp.stack([lines_ref[:, rt * 9 + j] for rt in range(3)], axis=1).reshape(N * 24, BX)

    def write(j, value):
        value = value.reshape(N, 3, 8, BX)
        for rt in range(3):
            lines_ref[:, rt * 9 + j] = value[:, rt]

    line_product(high_ref, low_ref, read, write)
    for r, route in enumerate(ROUTES):
        first, second = places(route, where_ref)
        tiles, width = tiles_of(route), len(route[2])
        for k2 in range(4):
            for k1 in range(4):
                target = device_at(route, (first - k1) % 4, (second - k2) % 4)
                for rt in range(3):
                    at = k1 * tiles + rt * width
                    outs[r * 4 + k2][at : at + width] = lines_ref[target, rt * 9 + route[2][0] : rt * 9 + route[2][0] + width]


def z_lines(where, arrays):
    high, low = z_matrix()
    shapes = []
    for route in ROUTES:
        shapes += [jax.ShapeDtypeStruct((4 * tiles_of(route), 8, BX), F32)] * 4
    return pl.pallas_call(
        z_kernel,
        in_specs=[SM] + [VM] * 10,
        out_specs=[VM] * 9,
        out_shape=shapes + [jax.ShapeDtypeStruct((8, BX), F32)],
        scratch_shapes=[pltpu.VMEM((N, 27, 8, BX), F32)],
        compiler_params=params(),
        name="z_lines",
    )(where, jnp.asarray(high), jnp.asarray(low), *arrays)


def z_unpack_kernel(where_ref, term_ref, *refs):
    out_ref, sum_ref = refs[8], refs[9]
    for r, route in enumerate(ROUTES):
        first, second = places(route, where_ref)
        width = len(route[2])
        for k1 in range(4):
            got = refs[r * 4 + k1]
            for k2 in range(4):
                device = device_at(route, (first + k1) % 4, (second + k2) % 4)
                for n, j in enumerate(route[2]):
                    y, low_cols = columns_of(device, j, 0)
                    y, high_cols = columns_of(device, j, 1)
                    base = k2 * 3 * width + n
                    for at, count, cols, tile, row in (
                        (0, 8, low_cols, base, 0),
                        (8, 4, low_cols, base + width, 0),
                        (0, 4, high_cols, base + width, 4),
                        (4, 8, high_cols, base + 2 * width, 0),
                    ):
                        spot = pl.ds(y + at * DY, count, stride=DY)
                        sum_ref[cols, spot, :] = got[tile, row : row + count]
    for xb in range(XB):
        cols = slice(xb * BX, xb * BX + BX)
        out_ref[:, cols] = term_ref[:, cols] + sum_ref[xb]


def z_unpack(where, term, arrays):
    return pl.pallas_call(
        z_unpack_kernel,
        in_specs=[SM] + [VM] * 9,
        out_specs=VM,
        out_shape=jax.ShapeDtypeStruct((DZ * DY, NX), F32),
        scratch_shapes=[pltpu.VMEM((XB, DZ * DY, BX), F32)],
        compiler_params=params(),
        name="z_unpack",
    )(where, term.reshape(DZ * DY, NX), *arrays).reshape(DZ, DY, NX)


def sigmoid(value):
    return 1.0 / (1.0 + jnp.exp(-value))


def axial(rel):
    return jnp.exp(-0.5 * (rel / DISK_DEPTH) ** 2)


def radial(rel_z, rel_y):
    return sigmoid((RADIUS * RADIUS - rel_y * rel_y - rel_z * rel_z) / (2.0 * RADIUS))


def disk_kernel(where_ref, brick_ref, offset_ref, wind_ref, lanes_ref, v_ref, sums_ref, denom_ref, disk_ref, slot_ref):
    level, column = where_ref[0], where_ref[3]
    sub = lax.broadcasted_iota(jnp.int32, (8, BX), 0).astype(F32)
    lane = lax.broadcasted_iota(jnp.int32, (8, BX), 1)
    top = lax.broadcasted_iota(jnp.int32, (8, BX), 0) == 0
    sums_ref[...] = jnp.zeros((8, BX), F32)

    centre_z, centre_y, centre_x = (lanes_ref[i : i + 1, :] for i in range(3))

    def add_radial(z, total):
        for yt in range(6):
            total = total + radial(z.astype(F32) - centre_z, sub + (8.0 * yt) - centre_y)
        return total

    area = jnp.sum(lax.fori_loop(0, 2 * DZ, add_radial, jnp.zeros((8, BX), F32)), axis=0, keepdims=True)
    depth = jnp.zeros((8, BX), F32)
    for xt in range(BX // 8):
        depth = depth + axial(sub + (8.0 * xt) - centre_x)
    denom_ref[...] = jnp.broadcast_to(area * jnp.sum(depth, axis=0, keepdims=True), (8, BX))

    for s in range(2 * XB):
        slot_ref[s] = -1

    @pl.when(level < 2)
    def _():
        def place(t, carry):
            base = brick_ref[t, 0]
            left, block = (base // XB) % N, base % XB
            shifted = column - left

            @pl.when((shifted == 0) | (shifted == 1))
            def _():
                slot_ref[shifted * XB + block] = t

            return carry

        lax.fori_loop(0, TURB, place, 0)

        def one(s, carry):
            k, block = s // XB, s % XB
            cols = pl.ds(pl.multiple_of(block * BX, BX), BX)
            t = slot_ref[s]

            @pl.when(t < 0)
            def _():
                for z in range(DZ):
                    disk_ref[k, z, :, cols] = jnp.zeros((DY, BX), F32)

            @pl.when(t >= 0)
            def _():
                base_z = (level * DZ - offset_ref[t, 0]).astype(F32)
                base_y = (k * DY - offset_ref[t, 1]).astype(F32)
                shape_x = axial((lane - offset_ref[t, 2]).astype(F32))
                total = jnp.zeros((8, BX), F32)
                for z in range(DZ):
                    for yt in range(3):
                        weight = shape_x * radial(base_z + float(z), sub + (base_y + 8.0 * yt))
                        disk_ref[k, z, yt * 8 : yt * 8 + 8, cols] = weight
                        total = total + weight * (wind_ref[z] + v_ref[z, yt * 8 : yt * 8 + 8, cols])
                found = jnp.sum(total)
                sums_ref[...] = sums_ref[...] + jnp.where((lane == t) & top, found, 0.0)

            return carry

        lax.fori_loop(0, 2 * XB, one, 0)


def disks(where, bricks, offset, wind, velocity):
    lanes = jnp.pad(offset.T.astype(F32), ((0, 5), (0, BX - TURB)))
    return pl.pallas_call(
        disk_kernel,
        in_specs=[SM, SM, SM, SM, VM, VM],
        out_specs=[VM, VM, VM, SM],
        out_shape=[
            jax.ShapeDtypeStruct((8, BX), F32),
            jax.ShapeDtypeStruct((8, BX), F32),
            jax.ShapeDtypeStruct((2, DZ, DY, NX), F32),
            jax.ShapeDtypeStruct((2 * XB,), jnp.int32),
        ],
        compiler_params=params(),
        name="disks",
    )(where, bricks, offset, wind, lanes, velocity)


def final_kernel(where_ref, slot_ref, terms_ref, lines_ref, sums_ref, denom_ref, coef_ref, disk_ref, out_ref, speed_ref, push_ref):
    level = where_ref[0]

    @pl.when(pl.program_id(0) == 0)
    def _():
        total = sums_ref[0, 0]
        for d in range(1, N):
            total = total + sums_ref[d, 0]
        speed = total[0:1, :] / denom_ref[0:1, :]
        speed_ref[...] = speed
        thrust = -0.5 * coef_ref[...] * speed * jnp.abs(speed)
        lane = lax.broadcasted_iota(jnp.int32, (1, BX), 1)
        for s in range(2 * XB):
            mine = jnp.sum(jnp.where(lane == slot_ref[s], thrust, 0.0), axis=1, keepdims=True)
            push_ref[s] = jnp.broadcast_to(mine, (8, BX))

    def cell(local, yt):
        z, xb = local // XB, local % XB
        rows, cols = slice(yt * 8, yt * 8 + 8), slice(xb * BX, xb * BX + BX)
        return z, xb, rows, cols, terms_ref[z, rows, cols] + lines_ref[local // 9, yt * 9 + local % 9]

    @pl.when(level < 2)
    def _():
        for local in range(36):
            for yt in range(3):
                z, xb, rows, cols, value = cell(local, yt)
                out_ref[z, rows, cols] = (
                    value
                    + push_ref[xb] * disk_ref[0, z, rows, cols]
                    + push_ref[XB + xb] * disk_ref[1, z, rows, cols]
                )

    @pl.when(level >= 2)
    def _():
        for local in range(36):
            for yt in range(3):
                z, xb, rows, cols, value = cell(local, yt)
                out_ref[z, rows, cols] = value


def finish(where, slots, terms, lines, denom, coef, disk):
    return pl.pallas_call(
        final_kernel,
        grid=(4,),
        in_specs=[
            SM,
            SM,
            pl.BlockSpec((3, DY, NX), lambda i: (i, 0, 0)),
            pl.BlockSpec((4, 28, 8, BX), lambda i: (i, 0, 0, 0)),
            pl.BlockSpec((N, 1, 8, BX), lambda i: (0, 27, 0, 0)),
            pl.BlockSpec((8, BX), lambda i: (0, 0)),
            pl.BlockSpec((1, BX), lambda i: (0, 0)),
            pl.BlockSpec((2, 3, DY, NX), lambda i: (0, i, 0, 0)),
        ],
        out_specs=[
            pl.BlockSpec((3, DY, NX), lambda i: (i, 0, 0)),
            pl.BlockSpec((1, BX), lambda i: (0, 0)),
        ],
        out_shape=[jax.ShapeDtypeStruct((DZ, DY, NX), F32), jax.ShapeDtypeStruct((1, BX), F32)],
        scratch_shapes=[pltpu.VMEM((2 * XB, 8, BX), F32)],
        compiler_params=params(),
        name="finish",
    )(where, slots, terms, lines, lines, denom, coef, disk)


def body(velocity, wind, thrust_coef, bricks, offset):
    pz, py = lax.axis_index("pz"), lax.axis_index("py")
    where = jnp.stack([pz, pz // 4, pz % 4, py]).astype(jnp.int32)
    with jax.named_scope("spanwise_send"):
        received = lax.all_to_all(y_pack(velocity), "py", 0, 0, tiled=True)
    sums, denom, disk, slots = disks(where, bricks, offset, wind, velocity)
    packed = z_pack(where, velocity, sums)
    with jax.named_scope("vertical_send"):
        arrived = []
        for r, route in enumerate(ROUTES):
            stage = send_stage(packed[4 * r : 4 * r + 4], route[0], 1)
            stage = regroup(stage, tiles_of(route), True)
            arrived += send_stage(stage, route[1], 1)
    term_x = along_x(velocity, wind)
    *vertical, level_sums = z_lines(where, arrived)
    spanwise = y_lines(received, level_sums)
    with jax.named_scope("spanwise_return"):
        returned = lax.all_to_all(spanwise, "py", 0, 0, tiled=True)
    with jax.named_scope("vertical_return"):
        back = []
        for r, route in enumerate(ROUTES):
            stage = send_stage(vertical[4 * r : 4 * r + 4], route[1], -1)
            stage = regroup(stage, tiles_of(route), False)
            back += send_stage(stage, route[0], -1)
    terms = z_unpack(where, term_x, back)
    coef = jnp.pad(thrust_coef, (0, BX - TURB)).reshape(1, BX)
    tendency, speed = finish(where, slots, terms, returned, denom, coef, disk)
    return tendency, speed[0, :TURB]


def solution(mesh):
    return jax.shard_map(
        body,
        mesh=mesh,
        in_specs=(P("pz", "py", None), P("pz"), P(), P(), P()),
        out_specs=(P("pz", "py", None), P()),
        check_vma=False,
    )
```

```python
import functools
import math

import jax
import jax.numpy as jnp
import ml_dtypes
import numpy as np
from jax import lax
from jax.experimental import pallas as pl
from jax.experimental.pallas import tpu as pltpu
from jax.sharding import PartitionSpec as P

NX, NY, NZ, BX = 1536, 384, 192, 128
TURB = 100
N = 16
DZ, DY, XB = NZ // N, NY // N, NX // BX
HALF = NX // 2
VISCOSITY = 0.2
CROSS_WIND = 0.4
DISK_DEPTH = 1.5
RADIUS = 0.6 * DZ
F32, BF16 = jnp.float32, jnp.bfloat16
VM = pl.BlockSpec(memory_space=pltpu.VMEM)
SM = pl.BlockSpec(memory_space=pltpu.SMEM)
HB = pl.BlockSpec(memory_space=pltpu.HBM)
ROUTES = (("x", "y", (0, 1, 2, 3, 4)), ("y", "x", (5, 6, 7, 8)))


WHOLE = 57


class Mover:
    def __init__(self, sems):
        self.sems, self.used = sems, 0

    def start(self, source, target):
        copy = pltpu.make_async_copy(source, target, self.sems.at[self.used])
        self.used += 1
        copy.start()
        return copy


def wait(copies):
    for copy in copies:
        copy.wait()


def params(mib=8):
    return pltpu.CompilerParams(vmem_limit_bytes=mib * 1024 * 1024)


def kernels_of(length):
    m = np.arange(length)
    m = np.where(m > length // 2, m - length, m).astype(np.float64)
    parity = np.where(m % 2 == 0, 1.0, -1.0)
    angle = math.pi / length * m
    sine = np.where(m == 0, 1.0, np.sin(angle))
    first = np.where(m == 0, 0.0, math.pi / length * parity * np.cos(angle) / sine)
    second = np.where(
        m == 0,
        -math.pi**2 / 3.0 - 2.0 * math.pi**2 / (3.0 * length * length),
        -(2.0 * math.pi**2 / (length * length)) * parity / (sine * sine),
    )
    return first, second


def split(table):
    high = table.astype(np.float32).astype(ml_dtypes.bfloat16)
    low = (table - high.astype(np.float64)).astype(np.float32).astype(ml_dtypes.bfloat16)
    return high, low


def x_tables():
    first, second = kernels_of(NX)
    source, target = np.arange(HALF)[:, None], np.arange(256)[None, :]
    near, far = (target - source) % NX, (target - source + HALF) % NX
    mats = []
    for sign in (1.0, -1.0):
        for table in (VISCOSITY * second, first):
            mats.extend(split(0.5 * (table[near] + sign * table[far])))
    return np.stack(mats)


def y_matrix():
    first, second = kernels_of(NY)
    i = np.arange(NY)
    return split((VISCOSITY * second - CROSS_WIND * first)[(i[:, None] - i[None, :]) % NY])


def z_matrix():
    _, second = kernels_of(NZ)
    row = np.arange(N * 2 * DZ)
    block, inner = row // (2 * DZ), row % (2 * DZ)
    half, height = inner // DZ, block * DZ + inner % DZ
    table = VISCOSITY * second[(height[:, None] - height[None, :]) % NZ]
    return split(np.where(half[:, None] == half[None, :], table, 0.0))


def halves(value):
    high = value.astype(BF16)
    return high, (value - high.astype(F32)).astype(BF16)


def dot(a, b):
    return jnp.dot(a, b, preferred_element_type=F32)


def x_kernel(wind_ref, offset_ref, v_ref, table_ref, out_ref, denom_ref, lhs_ref, hold_ref):
    rows = DZ * DY
    for part in range(2):
        for block in range(3):
            low_x = v_ref[:, :, block * 256 : block * 256 + 256].reshape(rows, 256)
            high_x = v_ref[:, :, HALF + block * 256 : HALF + block * 256 + 256].reshape(rows, 256)
            value = low_x + high_x if part == 0 else low_x - high_x
            for at, number in ((block, value), (block + 3, value if part == 0 else -value)):
                if at < 5:
                    high, low = halves(number)
                    lhs_ref[part, :rows, at * 256 : at * 256 + 256] = high
                    lhs_ref[part, rows:, at * 256 : at * 256 + 256] = low

    for step in range(3):
        terms = []
        for part in range(2):
            lhs = lhs_ref[part, :, step * 256 : step * 256 + HALF]
            got = []
            for which in range(2):
                both = dot(lhs, table_ref[4 * part + 2 * which])
                extra = dot(lhs[:rows], table_ref[4 * part + 2 * which + 1])
                got.append((both[:rows] + both[rows:] + extra).reshape(DZ, DY, 256))
            terms.append(got)
        here = slice(step * 256, step * 256 + 256)
        there = slice(HALF + step * 256, HALF + step * 256 + 256)
        for z in range(DZ):
            even = terms[0][0][z] - wind_ref[z] * terms[0][1][z]
            odd = terms[1][0][z] - wind_ref[z] * terms[1][1][z]
            out_ref[z, :, here] = even + odd
            out_ref[z, :, there] = even - odd

    hold_ref[...] = jnp.zeros((8, BX), F32)
    hold_ref[0:3, 0:TURB] = offset_ref[...].astype(F32)
    centre_z, centre_y, centre_x = (hold_ref[i : i + 1, :] for i in range(3))
    sub = lax.broadcasted_iota(jnp.int32, (8, BX), 0).astype(F32)

    def add_radial(z, total):
        for yt in range(6):
            total = total + radial(z.astype(F32) - centre_z, sub + (8.0 * yt) - centre_y)
        return total

    area = jnp.sum(lax.fori_loop(0, 2 * DZ, add_radial, jnp.zeros((8, BX), F32)), axis=0, keepdims=True)
    depth = jnp.zeros((8, BX), F32)
    for xt in range(BX // 8):
        depth = depth + axial(sub + (8.0 * xt) - centre_x)
    denom_ref[...] = jnp.broadcast_to(area * jnp.sum(depth, axis=0, keepdims=True), (8, BX))


def along_x(velocity, wind, offset):
    return pl.pallas_call(
        x_kernel,
        in_specs=[SM, VM, VM, VM],
        out_specs=[VM, VM],
        out_shape=[jax.ShapeDtypeStruct((DZ, DY, NX), F32), jax.ShapeDtypeStruct((8, BX), F32)],
        scratch_shapes=[pltpu.VMEM((2, 2 * DZ * DY, 1280), BF16), pltpu.VMEM((8, BX), F32)],
        compiler_params=params(24),
        cost_estimate=pl.CostEstimate(
            flops=2 * 288 * 768 * 768 * 12, bytes_accessed=7 * 2**20, transcendentals=0
        ),
        name="x_derivative",
    )(wind, offset.T, velocity, jnp.asarray(x_tables()))


def y_pack_kernel(v_ref, out_ref, from_ref, to_ref, in_sem, out_sem):
    into = [
        pltpu.make_async_copy(v_ref.at[pl.ds(z, 1)], from_ref.at[pl.ds(z, 1)], in_sem.at[z])
        for z in range(DZ)
    ]
    away = [
        pltpu.make_async_copy(to_ref.at[pl.ds(d, 1)], out_ref.at[pl.ds(d, 1)], out_sem.at[d])
        for d in range(N)
    ]
    for copy in into:
        copy.start()
    for pair in range(DZ * XB):
        z, xb, d, j = pair // XB, pair % XB, pair // 9, pair % 9
        if xb == 0:
            into[z].wait()
        for yt in range(3):
            to_ref[d, yt * 9 + j] = from_ref[z, yt * 8 : yt * 8 + 8, xb * BX : xb * BX + BX]
        if j == 8:
            away[d].start()
    wait(away)


def y_pack(velocity):
    return pl.pallas_call(
        y_pack_kernel,
        in_specs=[HB],
        out_specs=HB,
        out_shape=jax.ShapeDtypeStruct((N, 27, 8, BX), F32),
        scratch_shapes=[
            pltpu.VMEM((DZ, DY, NX), F32),
            pltpu.VMEM((N, 27, 8, BX), F32),
            pltpu.SemaphoreType.DMA((DZ,)),
            pltpu.SemaphoreType.DMA((N,)),
        ],
        compiler_params=params(WHOLE),
        name="y_pack",
    )(velocity)


def sums_kernel(*refs):
    sources, (out_ref, sums_ref, sems) = refs[:8], refs[9:]
    move = Mover(sems)
    last = 4 * tiles_of(ROUTES[0])
    wait([move.start(sources[i].at[last], sums_ref.at[i]) for i in range(4)])
    out_ref[...] = (sums_ref[0] + sums_ref[1]) + (sums_ref[2] + sums_ref[3])


def level_sums(arrived, term_x):
    return pl.pallas_call(
        sums_kernel,
        in_specs=[HB] * 9,
        out_specs=VM,
        out_shape=jax.ShapeDtypeStruct((8, BX), F32),
        scratch_shapes=[pltpu.VMEM((4, 8, BX), F32), pltpu.SemaphoreType.DMA((4,))],
        compiler_params=params(WHOLE),
        name="level_sums",
    )(*arrived, term_x)


def y_kernel(matrix_ref, sums_ref, in_ref, after_ref, out_ref):
    for group in range(3):
        tiles = []
        for j in range(3 * group, 3 * group + 3):
            tiles.append(jnp.stack([in_ref[:, yt * 9 + j] for yt in range(3)], axis=1).reshape(NY, BX))
        high, low = halves(jnp.concatenate(tiles, axis=1))
        got = dot(matrix_ref[0], high) + dot(matrix_ref[1], high) + dot(matrix_ref[0], low)
        for k in range(3):
            value = got[:, k * BX : k * BX + BX].reshape(N, 3, 8, BX)
            for yt in range(3):
                out_ref[:, yt * 9 + 3 * group + k] = value[:, yt]
    for d in range(N):
        out_ref[d, 27] = sums_ref[...]


def y_lines(sums, received, after):
    return pl.pallas_call(
        y_kernel,
        in_specs=[VM] * 3 + [HB],
        out_specs=VM,
        out_shape=jax.ShapeDtypeStruct((N, 28, 8, BX), F32),
        compiler_params=params(16),
        name="y_lines",
    )(jnp.asarray(np.stack(y_matrix())), sums, received, after)


def device_at(route, place_first, place_second):
    return place_first * 4 + place_second if route[0] == "x" else place_second * 4 + place_first


def places(route, where_ref):
    x, y = where_ref[1], where_ref[2]
    return (x, y) if route[0] == "x" else (y, x)


def tiles_of(route):
    return 3 * len(route[2])


def columns_of(device, j, h):
    y = (device // 2) * 3 + j // 3
    xb = ((device % 2) * 2 + h) * 3 + j % 3
    return y, xb


def z_pack_kernel(r, where_ref, in_ref, *refs):
    sums_ref, (*out_refs, v_ref) = refs[0], refs[-5:]
    for xb in range(XB):
        v_ref[xb] = in_ref[:, xb * BX : xb * BX + BX]
    route = ROUTES[r]
    first, second = places(route, where_ref)
    width = len(route[2])
    for k1 in range(4):
        out = out_refs[k1]
        if r == 0:
            out[4 * 3 * width] = sums_ref[...]
        for k2 in range(4):
            device = device_at(route, (first + k1) % 4, (second + k2) % 4)
            for n, j in enumerate(route[2]):
                y, low_cols = columns_of(device, j, 0)
                y, high_cols = columns_of(device, j, 1)
                base = k2 * 3 * width + n
                out[base] = v_ref[low_cols, pl.ds(y, 8, stride=DY), :]
                out[base + width, 0:4] = v_ref[low_cols, pl.ds(y + 8 * DY, 4, stride=DY), :]
                out[base + width, 4:8] = v_ref[high_cols, pl.ds(y, 4, stride=DY), :]
                out[base + 2 * width] = v_ref[high_cols, pl.ds(y + 4 * DY, 8, stride=DY), :]


def z_pack(r, where, velocity, sums):
    shape = jax.ShapeDtypeStruct((4 * tiles_of(ROUTES[r]) + (r == 0), 8, BX), F32)
    return pl.pallas_call(
        functools.partial(z_pack_kernel, r),
        in_specs=[SM, VM] + [VM] * (r == 0),
        out_specs=[VM] * 4,
        out_shape=[shape] * 4,
        scratch_shapes=[pltpu.VMEM((XB, DZ * DY, BX), F32)],
        compiler_params=params(),
        name="z_pack",
    )(where, velocity.reshape(DZ * DY, NX), *([sums] if r == 0 else []))


def regroup(arrays, tiles, with_sums):
    def kernel(*refs):
        for i in range(4):
            for k in range(4):
                refs[4 + i][k * tiles : (k + 1) * tiles] = refs[k][i * tiles : (i + 1) * tiles]
            if with_sums:
                last = 4 * tiles
                refs[4 + i][last] = (refs[0][last] + refs[1][last]) + (refs[2][last] + refs[3][last])

    shape = jax.ShapeDtypeStruct((4 * tiles + (1 if with_sums else 0), 8, BX), F32)
    return pl.pallas_call(
        kernel,
        in_specs=[VM] * 4,
        out_specs=[VM] * 4,
        out_shape=[shape] * 4,
        compiler_params=params(),
        name="regroup",
    )(*arrays)


def shift(value, axis, by):
    moves = []
    for i in range(N):
        x, y = i // 4, i % 4
        moves.append((i, ((x + by) % 4) * 4 + y if axis == "x" else x * 4 + (y + by) % 4))
    return lax.ppermute(value, "pz", moves)


def send_stage(arrays, axis, sign):
    return [arrays[0]] + [shift(arrays[k], axis, sign * k) for k in range(1, 4)]


def z_kernel(r, where_ref, matrix_hbm, *refs):
    ins_hbm, outs_hbm, refs = refs[:4], refs[5:9], refs[9:]
    ins, outs, (matrix_ref, lines_ref, sems) = refs[:4], refs[4:8], refs[8:]
    route = ROUTES[r]
    first, second = places(route, where_ref)
    tiles, width = tiles_of(route), len(route[2])
    move = Mover(sems)
    fetch = [move.start(ins_hbm[i], ins[i]) for i in range(4)]
    fetch_matrix = move.start(matrix_hbm, matrix_ref)
    away = []

    def spots(k2):
        for k1 in range(4):
            device = device_at(route, (first - k1) % 4, (second - k2) % 4)
            yield device, slice(k1 * tiles, (k1 + 1) * tiles)

    for k2 in range(4):
        fetch[k2].wait()
        for device, outer in spots(k2):
            lines_ref[device] = ins[k2][outer]
    columns = []
    for j in range(width):
        columns.append(jnp.stack([lines_ref[:, rt * width + j] for rt in range(3)], axis=1).reshape(N * 24, BX))
    high, low = halves(jnp.concatenate(columns, axis=1))
    fetch_matrix.wait()
    got = dot(matrix_ref[0], high) + dot(matrix_ref[1], high) + dot(matrix_ref[0], low)
    for j in range(width):
        value = got[:, j * BX : j * BX + BX].reshape(N, 3, 8, BX)
        for rt in range(3):
            lines_ref[:, rt * width + j] = value[:, rt]
    for k2 in range(4):
        for device, outer in spots(k2):
            outs[k2][outer] = lines_ref[device]
        away.append(move.start(outs[k2], outs_hbm[k2]))
    wait(away)


def z_lines(r, where, after, arrays):
    tiles = tiles_of(ROUTES[r])
    shapes = [jax.ShapeDtypeStruct((4 * tiles, 8, BX), F32)] * 4
    return pl.pallas_call(
        functools.partial(z_kernel, r),
        in_specs=[SM] + [HB] * 6,
        out_specs=[HB] * 4,
        out_shape=shapes,
        scratch_shapes=[pltpu.VMEM(a.shape, F32) for a in arrays]
        + [pltpu.VMEM(a.shape, F32) for a in shapes]
        + [
            pltpu.VMEM((2, N * 24, N * 24), BF16),
            pltpu.VMEM((N, tiles, 8, BX), F32),
            pltpu.SemaphoreType.DMA((9,)),
        ],
        compiler_params=params(WHOLE),
        name="z_lines",
    )(where, jnp.asarray(np.stack(z_matrix())), *arrays, after)


def z_unpack_kernel(where_ref, term_ref, *refs):
    out_ref, sum_ref = refs[8:]
    for r, route in enumerate(ROUTES):
        first, second = places(route, where_ref)
        width = len(route[2])
        for k1 in range(4):
            got = refs[r * 4 + k1]
            for k2 in range(4):
                device = device_at(route, (first + k1) % 4, (second + k2) % 4)
                for n, j in enumerate(route[2]):
                    y, low_cols = columns_of(device, j, 0)
                    y, high_cols = columns_of(device, j, 1)
                    base = k2 * 3 * width + n
                    for at, count, cols, tile, row in (
                        (0, 8, low_cols, base, 0),
                        (8, 4, low_cols, base + width, 0),
                        (0, 4, high_cols, base + width, 4),
                        (4, 8, high_cols, base + 2 * width, 0),
                    ):
                        spot = pl.ds(y + at * DY, count, stride=DY)
                        sum_ref[cols, spot, :] = got[tile, row : row + count]

    for xb in range(XB):
        cols = slice(xb * BX, xb * BX + BX)
        out_ref[:, cols] = term_ref[:, cols] + sum_ref[xb]


def z_unpack(where, term, arrays):
    return pl.pallas_call(
        z_unpack_kernel,
        in_specs=[SM] + [VM] * 9,
        out_specs=VM,
        out_shape=jax.ShapeDtypeStruct((DZ * DY, NX), F32),
        scratch_shapes=[pltpu.VMEM((XB, DZ * DY, BX), F32)],
        compiler_params=params(),
        name="z_unpack",
    )(where, term.reshape(DZ * DY, NX), *arrays).reshape(DZ, DY, NX)


def sigmoid(value):
    return 1.0 / (1.0 + jnp.exp(-value))


def axial(rel):
    return jnp.exp(-0.5 * (rel / DISK_DEPTH) ** 2)


def radial(rel_z, rel_y):
    return sigmoid((RADIUS * RADIUS - rel_y * rel_y - rel_z * rel_z) / (2.0 * RADIUS))


def disk_kernel(where_ref, wind_ref, brick_ref, offset_ref, v_ref, sums_ref, high_ref, low_ref, radial_ref, hold_ref, ahead_ref, behind_ref):
    level, column = where_ref[0], where_ref[3]
    sums_ref[...] = jnp.zeros((8, BX), F32)

    @pl.when(level < 2)
    def _():
        hold_ref[...] = jnp.zeros((8, BX), F32)
        hold_ref[0:1, 0:TURB] = brick_ref[0:1, :].astype(F32)
        hold_ref[1:4, 0:TURB] = offset_ref[...].astype(F32)
        brick, centre_z, centre_y, centre_x = (hold_ref[i : i + 1, :] for i in range(4))
        line = jnp.floor((brick + 0.5) * (1.0 / XB))
        block = brick - XB * line
        left = line - N * jnp.floor((line + 0.5) * (1.0 / N))
        shifted = column.astype(F32) - left
        lane = lax.broadcasted_iota(jnp.int32, (1, BX), 1)
        here = ((shifted == 0.0) | (shifted == 1.0)) & (lane < TURB)
        block = jnp.where(here, block, -1.0)
        sub = lax.broadcasted_iota(jnp.int32, (8, BX), 0).astype(F32)
        along = lax.broadcasted_iota(jnp.int32, (BX, BX), 0).astype(F32)
        shape_x = axial(along - centre_x)
        depth = jnp.sum(shape_x, axis=0, keepdims=True)
        for xb in range(XB):
            weight = jnp.where(block == float(xb), shape_x, 0.0)
            high, low = halves(weight)
            ahead_ref[xb * BX : xb * BX + BX] = high
            behind_ref[xb * BX : xb * BX + BX] = low
            high, low = halves(weight.T)
            high_ref[:, xb * BX : xb * BX + BX] = high
            low_ref[:, xb * BX : xb * BX + BX] = low
        high, low = halves(v_ref[...].reshape(DZ * DY, NX))
        along_disk = dot(high, ahead_ref[...]) + dot(low, ahead_ref[...]) + dot(high, behind_ref[...])
        base_z = (level * DZ).astype(F32) - centre_z
        base_y = shifted * float(DY) - centre_y
        total = jnp.zeros((8, BX), F32)
        for z in range(DZ):
            for yt in range(3):
                rows = slice(z * DY + yt * 8, z * DY + yt * 8 + 8)
                weight = jnp.where(here, radial(base_z + float(z), sub + (base_y + 8.0 * yt)), 0.0)
                radial_ref[rows] = weight
                total = total + weight * (along_disk[rows] + wind_ref[z] * depth)
        sums_ref[0:1] = jnp.sum(total, axis=0, keepdims=True)


def disks(where, wind, bricks, offset, velocity):
    return pl.pallas_call(
        disk_kernel,
        in_specs=[SM, SM, VM, VM, VM],
        out_specs=[VM] * 4,
        out_shape=[
            jax.ShapeDtypeStruct((8, BX), F32),
            jax.ShapeDtypeStruct((BX, NX), BF16),
            jax.ShapeDtypeStruct((BX, NX), BF16),
            jax.ShapeDtypeStruct((DZ * DY, BX), F32),
        ],
        scratch_shapes=[
            pltpu.VMEM((8, BX), F32),
            pltpu.VMEM((NX, BX), BF16),
            pltpu.VMEM((NX, BX), BF16),
        ],
        compiler_params=params(16),
        name="disks",
    )(where, wind, bricks.T, offset.T, velocity)


def final_kernel(where_ref, coef_ref, denom_ref, high_ref, low_ref, radial_ref, terms_ref, lines_ref, out_ref, speed_ref, held_ref, push_ref, sem):
    level = where_ref[0]
    total = lines_ref[0, 27]
    for d in range(1, N):
        total = total + lines_ref[d, 27]
    speed = total[0:1, :] / denom_ref[0:1, :]
    speed_ref[...] = speed[:, :TURB]

    def emit(force):
        copies = []
        for part in range(4):
            for local in range(36 * part, 36 * part + 36):
                z, xb = local // XB, local % XB
                cols = slice(xb * BX, xb * BX + BX)
                for yt in range(3):
                    rows = slice(yt * 8, yt * 8 + 8)
                    value = terms_ref[z, rows, cols] + lines_ref[local // 9, yt * 9 + local % 9]
                    if force is not None:
                        value = value + force[z * DY + yt * 8 : z * DY + yt * 8 + 8, cols]
                    held_ref[z, rows, cols] = value
            span = pl.ds(3 * part, 3)
            copies.append(pltpu.make_async_copy(held_ref.at[span], out_ref.at[span], sem.at[part]))
            copies[-1].start()
        for copy in copies:
            copy.wait()

    @pl.when(level < 2)
    def _():
        push_ref[...] = jnp.zeros((8, BX), F32)
        push_ref[0:1, :TURB] = -0.5 * coef_ref[...] * speed[:, :TURB] * jnp.abs(speed[:, :TURB])
        high, low = halves(radial_ref[...] * push_ref[0:1, :])
        emit(dot(high, high_ref[...]) + dot(low, high_ref[...]) + dot(high, low_ref[...]))

    @pl.when(level >= 2)
    def _():
        emit(None)


def finish(where, coef, denom, basis, terms, lines):
    tendency, speed = pl.pallas_call(
        final_kernel,
        in_specs=[SM] + [VM] * 7,
        out_specs=[HB, VM],
        out_shape=[jax.ShapeDtypeStruct((DZ, DY, NX), F32), jax.ShapeDtypeStruct((1, TURB), F32)],
        scratch_shapes=[
            pltpu.VMEM((DZ, DY, NX), F32),
            pltpu.VMEM((8, BX), F32),
            pltpu.SemaphoreType.DMA((4,)),
        ],
        compiler_params=params(16),
        name="finish",
    )(where, coef, denom, *basis, terms, lines)
    return tendency, speed.reshape(TURB)


def body(velocity, wind, thrust_coef, bricks, offset):
    pz, py = lax.axis_index("pz"), lax.axis_index("py")
    packed = y_pack(velocity)
    packed, pz, py = lax.optimization_barrier((packed, pz, py))
    where = jnp.stack([pz, pz // 4, pz % 4, py]).astype(jnp.int32)
    with jax.named_scope("spanwise_send"):
        received = lax.all_to_all(packed, "py", 0, 0, tiled=True)
    sums, *basis = disks(where, wind, bricks, offset, velocity)
    with jax.named_scope("vertical_send"):
        arrived = []
        for r, route in enumerate(ROUTES):
            stage = send_stage(z_pack(r, where, velocity, sums), route[0], 1)
            stage = regroup(stage, tiles_of(route), r == 0)
            arrived += send_stage(stage, route[1], 1)
    term_x, denom = along_x(velocity, wind, offset)
    turned = z_lines(1, where, term_x, arrived[4:])
    spanwise = y_lines(level_sums(arrived, term_x), received, turned[0])
    vertical = z_lines(0, where, spanwise, arrived[:4]) + turned
    with jax.named_scope("spanwise_return"):
        returned = lax.all_to_all(spanwise, "py", 0, 0, tiled=True)
    with jax.named_scope("vertical_return"):
        back = []
        for r, route in enumerate(ROUTES):
            stage = send_stage(vertical[4 * r : 4 * r + 4], route[1], -1)
            stage = regroup(stage, tiles_of(route), False)
            back += send_stage(stage, route[0], -1)
    terms = z_unpack(where, term_x, back)
    return finish(where, thrust_coef.reshape(1, TURB), denom, basis, terms, returned)


def solution(mesh):
    return jax.shard_map(
        body,
        mesh=mesh,
        in_specs=(P("pz", "py", None), P("pz"), P(), P(), P()),
        out_specs=(P("pz", "py", None), P()),
        check_vma=False,
    )
```

```python
import functools
import math

import jax
import jax.numpy as jnp
import ml_dtypes
import numpy as np
from jax import lax
from jax.experimental import pallas as pl
from jax.experimental.pallas import tpu as pltpu
from jax.sharding import PartitionSpec as P

NX, NY, NZ, BX = 1536, 384, 192, 128
TURB = 100
N = 16
DZ, DY, XB = NZ // N, NY // N, NX // BX
HALF = NX // 2
VISCOSITY = 0.2
CROSS_WIND = 0.4
DISK_DEPTH = 1.5
RADIUS = 0.6 * DZ
F32, BF16 = jnp.float32, jnp.bfloat16
VM = pl.BlockSpec(memory_space=pltpu.VMEM)
SM = pl.BlockSpec(memory_space=pltpu.SMEM)
HB = pl.BlockSpec(memory_space=pltpu.HBM)
ROUTES = (("x", "y", (0, 1, 2, 3, 4, 5)), ("y", "x", (6, 7, 8)))


WHOLE = 57


class Mover:
    def __init__(self, sems):
        self.sems, self.used = sems, 0

    def start(self, source, target):
        copy = pltpu.make_async_copy(source, target, self.sems.at[self.used])
        self.used += 1
        copy.start()
        return copy


def wait(copies):
    for copy in copies:
        copy.wait()


def params(mib=8):
    return pltpu.CompilerParams(vmem_limit_bytes=mib * 1024 * 1024)


def kernels_of(length):
    m = np.arange(length)
    m = np.where(m > length // 2, m - length, m).astype(np.float64)
    parity = np.where(m % 2 == 0, 1.0, -1.0)
    angle = math.pi / length * m
    sine = np.where(m == 0, 1.0, np.sin(angle))
    first = np.where(m == 0, 0.0, math.pi / length * parity * np.cos(angle) / sine)
    second = np.where(
        m == 0,
        -math.pi**2 / 3.0 - 2.0 * math.pi**2 / (3.0 * length * length),
        -(2.0 * math.pi**2 / (length * length)) * parity / (sine * sine),
    )
    return first, second


def split(table):
    high = table.astype(np.float32).astype(ml_dtypes.bfloat16)
    low = (table - high.astype(np.float64)).astype(np.float32).astype(ml_dtypes.bfloat16)
    return high, low


def x_tables():
    first, second = kernels_of(NX)
    source, target = np.arange(HALF)[:, None], np.arange(256)[None, :]
    near, far = (target - source) % NX, (target - source + HALF) % NX
    mats = []
    for sign in (1.0, -1.0):
        for table in (VISCOSITY * second, first):
            mats.extend(split(0.5 * (table[near] + sign * table[far])))
    return np.stack(mats)


def y_matrix():
    first, second = kernels_of(NY)
    i = np.arange(NY)
    return split((VISCOSITY * second - CROSS_WIND * first)[(i[:, None] - i[None, :]) % NY])


def z_matrix():
    _, second = kernels_of(NZ)
    row = np.arange(N * 2 * DZ)
    block, inner = row // (2 * DZ), row % (2 * DZ)
    half, height = inner // DZ, block * DZ + inner % DZ
    table = VISCOSITY * second[(height[:, None] - height[None, :]) % NZ]
    return split(np.where(half[:, None] == half[None, :], table, 0.0))


def halves(value):
    high = value.astype(BF16)
    return high, (value - high.astype(F32)).astype(BF16)


def dot(a, b):
    return jnp.dot(a, b, preferred_element_type=F32)


def x_kernel(wind_ref, offset_ref, v_ref, table_ref, out_ref, denom_ref, lhs_ref, hold_ref):
    rows = DZ * DY
    for part in range(2):
        for block in range(3):
            low_x = v_ref[:, :, block * 256 : block * 256 + 256].reshape(rows, 256)
            high_x = v_ref[:, :, HALF + block * 256 : HALF + block * 256 + 256].reshape(rows, 256)
            value = low_x + high_x if part == 0 else low_x - high_x
            for at, number in ((block, value), (block + 3, value if part == 0 else -value)):
                if at < 5:
                    high, low = halves(number)
                    lhs_ref[part, :rows, at * 256 : at * 256 + 256] = high
                    lhs_ref[part, rows:, at * 256 : at * 256 + 256] = low

    for step in range(3):
        terms = []
        for part in range(2):
            lhs = lhs_ref[part, :, step * 256 : step * 256 + HALF]
            got = []
            for which in range(2):
                both = dot(lhs, table_ref[4 * part + 2 * which])
                extra = dot(lhs[:rows], table_ref[4 * part + 2 * which + 1])
                got.append((both[:rows] + both[rows:] + extra).reshape(DZ, DY, 256))
            terms.append(got)
        here = slice(step * 256, step * 256 + 256)
        there = slice(HALF + step * 256, HALF + step * 256 + 256)
        for z in range(DZ):
            even = terms[0][0][z] - wind_ref[z] * terms[0][1][z]
            odd = terms[1][0][z] - wind_ref[z] * terms[1][1][z]
            out_ref[z, :, here] = even + odd
            out_ref[z, :, there] = even - odd

    hold_ref[...] = jnp.zeros((8, BX), F32)
    hold_ref[0:3, 0:TURB] = offset_ref[...].astype(F32)
    centre_z, centre_y, centre_x = (hold_ref[i : i + 1, :] for i in range(3))
    sub = lax.broadcasted_iota(jnp.int32, (8, BX), 0).astype(F32)

    def add_radial(z, total):
        for yt in range(6):
            total = total + radial(z.astype(F32) - centre_z, sub + (8.0 * yt) - centre_y)
        return total

    area = jnp.sum(lax.fori_loop(0, 2 * DZ, add_radial, jnp.zeros((8, BX), F32)), axis=0, keepdims=True)
    depth = jnp.zeros((8, BX), F32)
    for xt in range(BX // 8):
        depth = depth + axial(sub + (8.0 * xt) - centre_x)
    denom_ref[...] = jnp.broadcast_to(area * jnp.sum(depth, axis=0, keepdims=True), (8, BX))


def along_x(velocity, wind, offset):
    return pl.pallas_call(
        x_kernel,
        in_specs=[SM, VM, VM, VM],
        out_specs=[VM, VM],
        out_shape=[jax.ShapeDtypeStruct((DZ, DY, NX), F32), jax.ShapeDtypeStruct((8, BX), F32)],
        scratch_shapes=[pltpu.VMEM((2, 2 * DZ * DY, 1280), BF16), pltpu.VMEM((8, BX), F32)],
        compiler_params=params(24),
        cost_estimate=pl.CostEstimate(
            flops=2 * 288 * 768 * 768 * 12, bytes_accessed=7 * 2**20, transcendentals=0
        ),
        name="x_derivative",
    )(wind, offset.T, velocity, jnp.asarray(x_tables()))


def y_pack_kernel(v_ref, out_ref, from_ref, to_ref, in_sem, out_sem):
    parts = range(4)
    into = [
        pltpu.make_async_copy(v_ref.at[pl.ds(3 * c, 3)], from_ref.at[pl.ds(3 * c, 3)], in_sem.at[c])
        for c in parts
    ]
    away = [
        pltpu.make_async_copy(to_ref.at[pl.ds(4 * c, 4)], out_ref.at[pl.ds(4 * c, 4)], out_sem.at[c])
        for c in parts
    ]
    for c in parts:
        into[c].start()
    for c in parts:
        into[c].wait()
        for local in range(36 * c, 36 * c + 36):
            z, xb = local // XB, local % XB
            for yt in range(3):
                to_ref[local // 9, yt * 9 + local % 9] = from_ref[z, yt * 8 : yt * 8 + 8, xb * BX : xb * BX + BX]
        away[c].start()
    for c in parts:
        away[c].wait()


def y_pack(velocity):
    return pl.pallas_call(
        y_pack_kernel,
        in_specs=[HB],
        out_specs=HB,
        out_shape=jax.ShapeDtypeStruct((N, 27, 8, BX), F32),
        scratch_shapes=[
            pltpu.VMEM((DZ, DY, NX), F32),
            pltpu.VMEM((N, 27, 8, BX), F32),
            pltpu.SemaphoreType.DMA((4,)),
            pltpu.SemaphoreType.DMA((4,)),
        ],
        compiler_params=params(WHOLE),
        name="y_pack",
    )(velocity)


def sums_kernel(*refs):
    sources, (out_ref, sums_ref, sems) = refs[:8], refs[9:]
    move = Mover(sems)
    last = 4 * tiles_of(ROUTES[0])
    wait([move.start(sources[i].at[last], sums_ref.at[i]) for i in range(4)])
    out_ref[...] = (sums_ref[0] + sums_ref[1]) + (sums_ref[2] + sums_ref[3])


def level_sums(arrived, term_x):
    return pl.pallas_call(
        sums_kernel,
        in_specs=[HB] * 9,
        out_specs=VM,
        out_shape=jax.ShapeDtypeStruct((8, BX), F32),
        scratch_shapes=[pltpu.VMEM((4, 8, BX), F32), pltpu.SemaphoreType.DMA((4,))],
        compiler_params=params(WHOLE),
        name="level_sums",
    )(*arrived, term_x)


def y_kernel(matrix_ref, sums_ref, in_ref, after_ref, out_ref):
    for group in range(3):
        tiles = []
        for j in range(3 * group, 3 * group + 3):
            tiles.append(jnp.stack([in_ref[:, yt * 9 + j] for yt in range(3)], axis=1).reshape(NY, BX))
        high, low = halves(jnp.concatenate(tiles, axis=1))
        got = dot(matrix_ref[0], high) + dot(matrix_ref[1], high) + dot(matrix_ref[0], low)
        for k in range(3):
            value = got[:, k * BX : k * BX + BX].reshape(N, 3, 8, BX)
            for yt in range(3):
                out_ref[:, yt * 9 + 3 * group + k] = value[:, yt]
    for d in range(N):
        out_ref[d, 27] = sums_ref[...]


def y_lines(sums, received, after):
    return pl.pallas_call(
        y_kernel,
        in_specs=[VM] * 3 + [HB],
        out_specs=VM,
        out_shape=jax.ShapeDtypeStruct((N, 28, 8, BX), F32),
        compiler_params=params(16),
        name="y_lines",
    )(jnp.asarray(np.stack(y_matrix())), sums, received, after)


def device_at(route, place_first, place_second):
    return place_first * 4 + place_second if route[0] == "x" else place_second * 4 + place_first


def places(route, where_ref):
    x, y = where_ref[1], where_ref[2]
    return (x, y) if route[0] == "x" else (y, x)


def tiles_of(route):
    return 3 * len(route[2])


def columns_of(device, j, h):
    y = (device // 2) * 3 + j // 3
    xb = ((device % 2) * 2 + h) * 3 + j % 3
    return y, xb


def z_pack_kernel(r, where_ref, in_ref, *refs):
    sums_ref, (*out_refs, v_ref) = refs[0], refs[-5:]
    for xb in range(XB):
        v_ref[xb] = in_ref[:, xb * BX : xb * BX + BX]
    route = ROUTES[r]
    first, second = places(route, where_ref)
    width = len(route[2])
    for k1 in range(4):
        out = out_refs[k1]
        if r == 0:
            out[4 * 3 * width] = sums_ref[...]
        for k2 in range(4):
            device = device_at(route, (first + k1) % 4, (second + k2) % 4)
            for n, j in enumerate(route[2]):
                y, low_cols = columns_of(device, j, 0)
                y, high_cols = columns_of(device, j, 1)
                base = k2 * 3 * width + n
                out[base] = v_ref[low_cols, pl.ds(y, 8, stride=DY), :]
                out[base + width, 0:4] = v_ref[low_cols, pl.ds(y + 8 * DY, 4, stride=DY), :]
                out[base + width, 4:8] = v_ref[high_cols, pl.ds(y, 4, stride=DY), :]
                out[base + 2 * width] = v_ref[high_cols, pl.ds(y + 4 * DY, 8, stride=DY), :]


def z_pack(r, where, velocity, sums):
    shape = jax.ShapeDtypeStruct((4 * tiles_of(ROUTES[r]) + (r == 0), 8, BX), F32)
    return pl.pallas_call(
        functools.partial(z_pack_kernel, r),
        in_specs=[SM, VM] + [VM] * (r == 0),
        out_specs=[VM] * 4,
        out_shape=[shape] * 4,
        scratch_shapes=[pltpu.VMEM((XB, DZ * DY, BX), F32)],
        compiler_params=params(),
        name="z_pack",
    )(where, velocity.reshape(DZ * DY, NX), *([sums] if r == 0 else []))


def regroup(arrays, tiles, with_sums):
    def kernel(*refs):
        for i in range(4):
            for k in range(4):
                refs[4 + i][k * tiles : (k + 1) * tiles] = refs[k][i * tiles : (i + 1) * tiles]
            if with_sums:
                last = 4 * tiles
                refs[4 + i][last] = (refs[0][last] + refs[1][last]) + (refs[2][last] + refs[3][last])

    shape = jax.ShapeDtypeStruct((4 * tiles + (1 if with_sums else 0), 8, BX), F32)
    return pl.pallas_call(
        kernel,
        in_specs=[VM] * 4,
        out_specs=[VM] * 4,
        out_shape=[shape] * 4,
        compiler_params=params(),
        name="regroup",
    )(*arrays)


def shift(value, axis, by):
    moves = []
    for i in range(N):
        x, y = i // 4, i % 4
        moves.append((i, ((x + by) % 4) * 4 + y if axis == "x" else x * 4 + (y + by) % 4))
    return lax.ppermute(value, "pz", moves)


def send_stage(arrays, axis, sign):
    return [arrays[0]] + [shift(arrays[k], axis, sign * k) for k in range(1, 4)]


def z_kernel(r, where_ref, matrix_hbm, *refs):
    ins_hbm, outs_hbm, refs = refs[:4], refs[5:9], refs[9:]
    ins, outs, (matrix_ref, lines_ref, sems) = refs[:4], refs[4:8], refs[8:]
    route = ROUTES[r]
    first, second = places(route, where_ref)
    tiles, width = tiles_of(route), len(route[2])
    move = Mover(sems)
    fetch = [move.start(ins_hbm[i], ins[i]) for i in range(4)]
    fetch_matrix = move.start(matrix_hbm, matrix_ref)
    away = []

    def spots(k2):
        for k1 in range(4):
            device = device_at(route, (first - k1) % 4, (second - k2) % 4)
            yield device, slice(k1 * tiles, (k1 + 1) * tiles)

    for k2 in range(4):
        fetch[k2].wait()
        for device, outer in spots(k2):
            lines_ref[device] = ins[k2][outer]
    columns = []
    for j in range(width):
        columns.append(jnp.stack([lines_ref[:, rt * width + j] for rt in range(3)], axis=1).reshape(N * 24, BX))
    high, low = halves(jnp.concatenate(columns, axis=1))
    fetch_matrix.wait()
    got = dot(matrix_ref[0], high) + dot(matrix_ref[1], high) + dot(matrix_ref[0], low)
    for j in range(width):
        value = got[:, j * BX : j * BX + BX].reshape(N, 3, 8, BX)
        for rt in range(3):
            lines_ref[:, rt * width + j] = value[:, rt]
    for k2 in range(4):
        for device, outer in spots(k2):
            outs[k2][outer] = lines_ref[device]
        away.append(move.start(outs[k2], outs_hbm[k2]))
    wait(away)


def z_lines(r, where, after, arrays):
    tiles = tiles_of(ROUTES[r])
    shapes = [jax.ShapeDtypeStruct((4 * tiles, 8, BX), F32)] * 4
    return pl.pallas_call(
        functools.partial(z_kernel, r),
        in_specs=[SM] + [HB] * 6,
        out_specs=[HB] * 4,
        out_shape=shapes,
        scratch_shapes=[pltpu.VMEM(a.shape, F32) for a in arrays]
        + [pltpu.VMEM(a.shape, F32) for a in shapes]
        + [
            pltpu.VMEM((2, N * 24, N * 24), BF16),
            pltpu.VMEM((N, tiles, 8, BX), F32),
            pltpu.SemaphoreType.DMA((9,)),
        ],
        compiler_params=params(WHOLE),
        name="z_lines",
    )(where, jnp.asarray(np.stack(z_matrix())), *arrays, after)


def z_unpack_kernel(where_ref, term_ref, *refs):
    out_ref, sum_ref = refs[8:]
    for r, route in enumerate(ROUTES):
        first, second = places(route, where_ref)
        width = len(route[2])
        for k1 in range(4):
            got = refs[r * 4 + k1]
            for k2 in range(4):
                device = device_at(route, (first + k1) % 4, (second + k2) % 4)
                for n, j in enumerate(route[2]):
                    y, low_cols = columns_of(device, j, 0)
                    y, high_cols = columns_of(device, j, 1)
                    base = k2 * 3 * width + n
                    for at, count, cols, tile, row in (
                        (0, 8, low_cols, base, 0),
                        (8, 4, low_cols, base + width, 0),
                        (0, 4, high_cols, base + width, 4),
                        (4, 8, high_cols, base + 2 * width, 0),
                    ):
                        spot = pl.ds(y + at * DY, count, stride=DY)
                        sum_ref[cols, spot, :] = got[tile, row : row + count]

    for xb in range(XB):
        cols = slice(xb * BX, xb * BX + BX)
        out_ref[:, cols] = term_ref[:, cols] + sum_ref[xb]


def z_unpack(where, term, arrays):
    return pl.pallas_call(
        z_unpack_kernel,
        in_specs=[SM] + [VM] * 9,
        out_specs=VM,
        out_shape=jax.ShapeDtypeStruct((DZ * DY, NX), F32),
        scratch_shapes=[pltpu.VMEM((XB, DZ * DY, BX), F32)],
        compiler_params=params(),
        name="z_unpack",
    )(where, term.reshape(DZ * DY, NX), *arrays).reshape(DZ, DY, NX)


def sigmoid(value):
    return 1.0 / (1.0 + jnp.exp(-value))


def axial(rel):
    return jnp.exp(-0.5 * (rel / DISK_DEPTH) ** 2)


def radial(rel_z, rel_y):
    return sigmoid((RADIUS * RADIUS - rel_y * rel_y - rel_z * rel_z) / (2.0 * RADIUS))


def disk_kernel(where_ref, wind_ref, brick_ref, offset_ref, v_ref, sums_ref, high_ref, low_ref, radial_ref, hold_ref, ahead_ref, behind_ref):
    level, column = where_ref[0], where_ref[3]
    sums_ref[...] = jnp.zeros((8, BX), F32)

    @pl.when(level < 2)
    def _():
        hold_ref[...] = jnp.zeros((8, BX), F32)
        hold_ref[0:1, 0:TURB] = brick_ref[0:1, :].astype(F32)
        hold_ref[1:4, 0:TURB] = offset_ref[...].astype(F32)
        brick, centre_z, centre_y, centre_x = (hold_ref[i : i + 1, :] for i in range(4))
        line = jnp.floor((brick + 0.5) * (1.0 / XB))
        block = brick - XB * line
        left = line - N * jnp.floor((line + 0.5) * (1.0 / N))
        shifted = column.astype(F32) - left
        lane = lax.broadcasted_iota(jnp.int32, (1, BX), 1)
        here = ((shifted == 0.0) | (shifted == 1.0)) & (lane < TURB)
        block = jnp.where(here, block, -1.0)
        sub = lax.broadcasted_iota(jnp.int32, (8, BX), 0).astype(F32)
        along = lax.broadcasted_iota(jnp.int32, (BX, BX), 0).astype(F32)
        shape_x = axial(along - centre_x)
        depth = jnp.sum(shape_x, axis=0, keepdims=True)
        for xb in range(XB):
            weight = jnp.where(block == float(xb), shape_x, 0.0)
            high, low = halves(weight)
            ahead_ref[xb * BX : xb * BX + BX] = high
            behind_ref[xb * BX : xb * BX + BX] = low
            high, low = halves(weight.T)
            high_ref[:, xb * BX : xb * BX + BX] = high
            low_ref[:, xb * BX : xb * BX + BX] = low
        high, low = halves(v_ref[...].reshape(DZ * DY, NX))
        along_disk = dot(high, ahead_ref[...]) + dot(low, ahead_ref[...]) + dot(high, behind_ref[...])
        base_z = (level * DZ).astype(F32) - centre_z
        base_y = shifted * float(DY) - centre_y
        total = jnp.zeros((8, BX), F32)
        for z in range(DZ):
            for yt in range(3):
                rows = slice(z * DY + yt * 8, z * DY + yt * 8 + 8)
                weight = jnp.where(here, radial(base_z + float(z), sub + (base_y + 8.0 * yt)), 0.0)
                radial_ref[rows] = weight
                total = total + weight * (along_disk[rows] + wind_ref[z] * depth)
        sums_ref[0:1] = jnp.sum(total, axis=0, keepdims=True)


def disks(where, wind, bricks, offset, velocity):
    return pl.pallas_call(
        disk_kernel,
        in_specs=[SM, SM, VM, VM, VM],
        out_specs=[VM] * 4,
        out_shape=[
            jax.ShapeDtypeStruct((8, BX), F32),
            jax.ShapeDtypeStruct((BX, NX), BF16),
            jax.ShapeDtypeStruct((BX, NX), BF16),
            jax.ShapeDtypeStruct((DZ * DY, BX), F32),
        ],
        scratch_shapes=[
            pltpu.VMEM((8, BX), F32),
            pltpu.VMEM((NX, BX), BF16),
            pltpu.VMEM((NX, BX), BF16),
        ],
        compiler_params=params(16),
        name="disks",
    )(where, wind, bricks.T, offset.T, velocity)


def final_kernel(where_ref, coef_ref, denom_ref, high_ref, low_ref, radial_ref, terms_ref, lines_ref, out_ref, speed_ref, held_ref, push_ref, sem):
    level = where_ref[0]
    total = lines_ref[0, 27]
    for d in range(1, N):
        total = total + lines_ref[d, 27]
    speed = total[0:1, :] / denom_ref[0:1, :]
    speed_ref[...] = speed[:, :TURB]

    def emit(force):
        copies = []
        for part in range(4):
            for local in range(36 * part, 36 * part + 36):
                z, xb = local // XB, local % XB
                cols = slice(xb * BX, xb * BX + BX)
                for yt in range(3):
                    rows = slice(yt * 8, yt * 8 + 8)
                    value = terms_ref[z, rows, cols] + lines_ref[local // 9, yt * 9 + local % 9]
                    if force is not None:
                        value = value + force[z * DY + yt * 8 : z * DY + yt * 8 + 8, cols]
                    held_ref[z, rows, cols] = value
            span = pl.ds(3 * part, 3)
            copies.append(pltpu.make_async_copy(held_ref.at[span], out_ref.at[span], sem.at[part]))
            copies[-1].start()
        for copy in copies:
            copy.wait()

    @pl.when(level < 2)
    def _():
        push_ref[...] = jnp.zeros((8, BX), F32)
        push_ref[0:1, :TURB] = -0.5 * coef_ref[...] * speed[:, :TURB] * jnp.abs(speed[:, :TURB])
        high, low = halves(radial_ref[...] * push_ref[0:1, :])
        emit(dot(high, high_ref[...]) + dot(low, high_ref[...]) + dot(high, low_ref[...]))

    @pl.when(level >= 2)
    def _():
        emit(None)


def finish(where, coef, denom, basis, terms, lines):
    tendency, speed = pl.pallas_call(
        final_kernel,
        in_specs=[SM] + [VM] * 7,
        out_specs=[HB, VM],
        out_shape=[jax.ShapeDtypeStruct((DZ, DY, NX), F32), jax.ShapeDtypeStruct((1, TURB), F32)],
        scratch_shapes=[
            pltpu.VMEM((DZ, DY, NX), F32),
            pltpu.VMEM((8, BX), F32),
            pltpu.SemaphoreType.DMA((4,)),
        ],
        compiler_params=params(16),
        name="finish",
    )(where, coef, denom, *basis, terms, lines)
    return tendency, speed.reshape(TURB)


def body(velocity, wind, thrust_coef, bricks, offset):
    pz, py = lax.axis_index("pz"), lax.axis_index("py")
    packed = y_pack(velocity)
    packed, pz, py = lax.optimization_barrier((packed, pz, py))
    where = jnp.stack([pz, pz // 4, pz % 4, py]).astype(jnp.int32)
    with jax.named_scope("spanwise_send"):
        received = lax.all_to_all(packed, "py", 0, 0, tiled=True)
    sums, *basis = disks(where, wind, bricks, offset, velocity)
    with jax.named_scope("vertical_send"):
        arrived = []
        for r, route in enumerate(ROUTES):
            stage = send_stage(z_pack(r, where, velocity, sums), route[0], 1)
            stage = regroup(stage, tiles_of(route), r == 0)
            arrived += send_stage(stage, route[1], 1)
    term_x, denom = along_x(velocity, wind, offset)
    turned = z_lines(1, where, term_x, arrived[4:])
    spanwise = y_lines(level_sums(arrived, term_x), received, turned[0])
    vertical = z_lines(0, where, spanwise, arrived[:4]) + turned
    with jax.named_scope("spanwise_return"):
        returned = lax.all_to_all(spanwise, "py", 0, 0, tiled=True)
    with jax.named_scope("vertical_return"):
        back = []
        for r, route in enumerate(ROUTES):
            stage = send_stage(vertical[4 * r : 4 * r + 4], route[1], -1)
            stage = regroup(stage, tiles_of(route), False)
            back += send_stage(stage, route[0], -1)
    terms = z_unpack(where, term_x, back)
    return finish(where, thrust_coef.reshape(1, TURB), denom, basis, terms, returned)


def solution(mesh):
    return jax.shard_map(
        body,
        mesh=mesh,
        in_specs=(P("pz", "py", None), P("pz"), P(), P(), P()),
        out_specs=(P("pz", "py", None), P()),
        check_vma=False,
    )
```

```python
import functools
import math

import jax
import jax.numpy as jnp
import ml_dtypes
import numpy as np
from jax import lax
from jax.experimental import pallas as pl
from jax.experimental.pallas import tpu as pltpu
from jax.sharding import PartitionSpec as P

NX, NY, NZ, BX = 1536, 384, 192, 128
TURB = 100
N = 16
DZ, DY, XB = NZ // N, NY // N, NX // BX
HALF = NX // 2
VISCOSITY = 0.2
CROSS_WIND = 0.4
DISK_DEPTH = 1.5
RADIUS = 0.6 * DZ
F32, BF16 = jnp.float32, jnp.bfloat16
VM = pl.BlockSpec(memory_space=pltpu.VMEM)
SM = pl.BlockSpec(memory_space=pltpu.SMEM)
HB = pl.BlockSpec(memory_space=pltpu.HBM)
ROUTES = (("x", "y", (0, 1, 2, 3, 4)), ("y", "x", (5, 6, 7, 8)))


WHOLE = 56


class Mover:
    def __init__(self, sems):
        self.sems, self.used = sems, 0

    def start(self, source, target):
        copy = pltpu.make_async_copy(source, target, self.sems.at[self.used])
        self.used += 1
        copy.start()
        return copy


def wait(copies):
    for copy in copies:
        copy.wait()


def params(mib=8):
    return pltpu.CompilerParams(vmem_limit_bytes=mib * 1024 * 1024)


def kernels_of(length):
    m = np.arange(length)
    m = np.where(m > length // 2, m - length, m).astype(np.float64)
    parity = np.where(m % 2 == 0, 1.0, -1.0)
    angle = math.pi / length * m
    sine = np.where(m == 0, 1.0, np.sin(angle))
    first = np.where(m == 0, 0.0, math.pi / length * parity * np.cos(angle) / sine)
    second = np.where(
        m == 0,
        -math.pi**2 / 3.0 - 2.0 * math.pi**2 / (3.0 * length * length),
        -(2.0 * math.pi**2 / (length * length)) * parity / (sine * sine),
    )
    return first, second


def split(table):
    high = table.astype(np.float32).astype(ml_dtypes.bfloat16)
    low = (table - high.astype(np.float64)).astype(np.float32).astype(ml_dtypes.bfloat16)
    return high, low


def x_tables():
    first, second = kernels_of(NX)
    source, target = np.arange(HALF)[:, None], np.arange(256)[None, :]
    near, far = (target - source) % NX, (target - source + HALF) % NX
    mats = []
    for sign in (1.0, -1.0):
        for table in (VISCOSITY * second, first):
            mats.extend(split(0.5 * (table[near] + sign * table[far])))
    return np.stack(mats)


def y_matrix():
    first, second = kernels_of(NY)
    i = np.arange(NY)
    return split((VISCOSITY * second - CROSS_WIND * first)[(i[:, None] - i[None, :]) % NY])


def z_matrix():
    _, second = kernels_of(NZ)
    row = np.arange(N * 2 * DZ)
    block, inner = row // (2 * DZ), row % (2 * DZ)
    half, height = inner // DZ, block * DZ + inner % DZ
    table = VISCOSITY * second[(height[:, None] - height[None, :]) % NZ]
    return split(np.where(half[:, None] == half[None, :], table, 0.0))


def halves(value):
    high = value.astype(BF16)
    return high, (value - high.astype(F32)).astype(BF16)


def dot(a, b):
    return jnp.dot(a, b, preferred_element_type=F32)


def x_kernel(wind_ref, offset_ref, v_ref, table_ref, out_ref, denom_ref, lhs_ref, hold_ref):
    rows = DZ * DY
    for part in range(2):
        for block in range(3):
            low_x = v_ref[:, :, block * 256 : block * 256 + 256].reshape(rows, 256)
            high_x = v_ref[:, :, HALF + block * 256 : HALF + block * 256 + 256].reshape(rows, 256)
            value = low_x + high_x if part == 0 else low_x - high_x
            for at, number in ((block, value), (block + 3, value if part == 0 else -value)):
                if at < 5:
                    high, low = halves(number)
                    lhs_ref[part, :rows, at * 256 : at * 256 + 256] = high
                    lhs_ref[part, rows:, at * 256 : at * 256 + 256] = low

    for step in range(3):
        terms = []
        for part in range(2):
            lhs = lhs_ref[part, :, step * 256 : step * 256 + HALF]
            got = []
            for which in range(2):
                both = dot(lhs, table_ref[4 * part + 2 * which])
                extra = dot(lhs[:rows], table_ref[4 * part + 2 * which + 1])
                got.append((both[:rows] + both[rows:] + extra).reshape(DZ, DY, 256))
            terms.append(got)
        here = slice(step * 256, step * 256 + 256)
        there = slice(HALF + step * 256, HALF + step * 256 + 256)
        for z in range(DZ):
            even = terms[0][0][z] - wind_ref[z] * terms[0][1][z]
            odd = terms[1][0][z] - wind_ref[z] * terms[1][1][z]
            out_ref[z, :, here] = even + odd
            out_ref[z, :, there] = even - odd

    hold_ref[...] = jnp.zeros((8, BX), F32)
    hold_ref[0:3, 0:TURB] = offset_ref[...].astype(F32)
    centre_z, centre_y, centre_x = (hold_ref[i : i + 1, :] for i in range(3))
    sub = lax.broadcasted_iota(jnp.int32, (8, BX), 0).astype(F32)

    def add_radial(z, total):
        for yt in range(6):
            total = total + radial(z.astype(F32) - centre_z, sub + (8.0 * yt) - centre_y)
        return total

    area = jnp.sum(lax.fori_loop(0, 2 * DZ, add_radial, jnp.zeros((8, BX), F32)), axis=0, keepdims=True)
    depth = jnp.zeros((8, BX), F32)
    for xt in range(BX // 8):
        depth = depth + axial(sub + (8.0 * xt) - centre_x)
    denom_ref[...] = jnp.broadcast_to(area * jnp.sum(depth, axis=0, keepdims=True), (8, BX))


def along_x(velocity, wind, offset):
    return pl.pallas_call(
        x_kernel,
        in_specs=[SM, VM, VM, VM],
        out_specs=[VM, VM],
        out_shape=[jax.ShapeDtypeStruct((DZ, DY, NX), F32), jax.ShapeDtypeStruct((8, BX), F32)],
        scratch_shapes=[pltpu.VMEM((2, 2 * DZ * DY, 1280), BF16), pltpu.VMEM((8, BX), F32)],
        compiler_params=params(24),
        cost_estimate=pl.CostEstimate(
            flops=2 * 288 * 768 * 768 * 12, bytes_accessed=7 * 2**20, transcendentals=0
        ),
        name="x_derivative",
    )(wind, offset.T, velocity, jnp.asarray(x_tables()))


def y_pack_kernel(v_ref, out_ref, from_ref, to_ref, in_sem, out_sem):
    parts = range(4)
    into = [
        pltpu.make_async_copy(v_ref.at[pl.ds(3 * c, 3)], from_ref.at[pl.ds(3 * c, 3)], in_sem.at[c])
        for c in parts
    ]
    away = [
        pltpu.make_async_copy(to_ref.at[pl.ds(4 * c, 4)], out_ref.at[pl.ds(4 * c, 4)], out_sem.at[c])
        for c in parts
    ]
    for c in parts:
        into[c].start()
    for c in parts:
        into[c].wait()
        for local in range(36 * c, 36 * c + 36):
            z, xb = local // XB, local % XB
            for yt in range(3):
                to_ref[local // 9, yt * 9 + local % 9] = from_ref[z, yt * 8 : yt * 8 + 8, xb * BX : xb * BX + BX]
        away[c].start()
    for c in parts:
        away[c].wait()


def y_pack(velocity):
    return pl.pallas_call(
        y_pack_kernel,
        in_specs=[HB],
        out_specs=HB,
        out_shape=jax.ShapeDtypeStruct((N, 27, 8, BX), F32),
        scratch_shapes=[
            pltpu.VMEM((DZ, DY, NX), F32),
            pltpu.VMEM((N, 27, 8, BX), F32),
            pltpu.SemaphoreType.DMA((4,)),
            pltpu.SemaphoreType.DMA((4,)),
        ],
        compiler_params=params(WHOLE),
        name="y_pack",
    )(velocity)


def sums_kernel(*refs):
    sources, (out_ref, sums_ref, sems) = refs[:8], refs[8:]
    move = Mover(sems)
    last = 4 * tiles_of(ROUTES[0])
    wait([move.start(sources[i].at[last], sums_ref.at[i]) for i in range(4)])
    out_ref[...] = (sums_ref[0] + sums_ref[1]) + (sums_ref[2] + sums_ref[3])


def level_sums(arrived):
    return pl.pallas_call(
        sums_kernel,
        in_specs=[HB] * 8,
        out_specs=VM,
        out_shape=jax.ShapeDtypeStruct((8, BX), F32),
        scratch_shapes=[pltpu.VMEM((4, 8, BX), F32), pltpu.SemaphoreType.DMA((4,))],
        compiler_params=params(),
        name="level_sums",
    )(*arrived)


def y_kernel(matrix_ref, sums_ref, in_ref, out_ref, done_ref):
    for group in range(3):
        tiles = []
        for j in range(3 * group, 3 * group + 3):
            tiles.append(jnp.stack([in_ref[:, yt * 9 + j] for yt in range(3)], axis=1).reshape(NY, BX))
        high, low = halves(jnp.concatenate(tiles, axis=1))
        got = dot(matrix_ref[0], high) + dot(matrix_ref[1], high) + dot(matrix_ref[0], low)
        for k in range(3):
            value = got[:, k * BX : k * BX + BX].reshape(N, 3, 8, BX)
            for yt in range(3):
                out_ref[:, yt * 9 + 3 * group + k] = value[:, yt]
    for d in range(N):
        out_ref[d, 27] = sums_ref[...]
    done_ref[...] = sums_ref[...]


def y_lines(sums, received):
    return pl.pallas_call(
        y_kernel,
        in_specs=[VM] * 3,
        out_specs=[VM] * 2,
        out_shape=[jax.ShapeDtypeStruct((N, 28, 8, BX), F32), jax.ShapeDtypeStruct((8, BX), F32)],
        compiler_params=params(16),
        name="y_lines",
    )(jnp.asarray(np.stack(y_matrix())), sums, received)


def device_at(route, place_first, place_second):
    return place_first * 4 + place_second if route[0] == "x" else place_second * 4 + place_first


def places(route, where_ref):
    x, y = where_ref[1], where_ref[2]
    return (x, y) if route[0] == "x" else (y, x)


def tiles_of(route):
    return 3 * len(route[2])


def columns_of(device, j, h):
    y = (device // 2) * 3 + j // 3
    xb = ((device % 2) * 2 + h) * 3 + j % 3
    return y, xb


def z_pack_kernel(r, where_ref, in_ref, *refs):
    sums_ref, (*out_refs, v_ref) = refs[0], refs[-5:]
    for xb in range(XB):
        v_ref[xb] = in_ref[:, xb * BX : xb * BX + BX]
    route = ROUTES[r]
    first, second = places(route, where_ref)
    width = len(route[2])
    for k1 in range(4):
        out = out_refs[k1]
        if r == 0:
            out[4 * 3 * width] = sums_ref[...]
        for k2 in range(4):
            device = device_at(route, (first + k1) % 4, (second + k2) % 4)
            for n, j in enumerate(route[2]):
                y, low_cols = columns_of(device, j, 0)
                y, high_cols = columns_of(device, j, 1)
                base = k2 * 3 * width + n
                out[base] = v_ref[low_cols, pl.ds(y, 8, stride=DY), :]
                out[base + width, 0:4] = v_ref[low_cols, pl.ds(y + 8 * DY, 4, stride=DY), :]
                out[base + width, 4:8] = v_ref[high_cols, pl.ds(y, 4, stride=DY), :]
                out[base + 2 * width] = v_ref[high_cols, pl.ds(y + 4 * DY, 8, stride=DY), :]


def z_pack(r, where, velocity, sums):
    shape = jax.ShapeDtypeStruct((4 * tiles_of(ROUTES[r]) + (r == 0), 8, BX), F32)
    return pl.pallas_call(
        functools.partial(z_pack_kernel, r),
        in_specs=[SM, VM] + [VM] * (r == 0),
        out_specs=[VM] * 4,
        out_shape=[shape] * 4,
        scratch_shapes=[pltpu.VMEM((XB, DZ * DY, BX), F32)],
        compiler_params=params(),
        name="z_pack",
    )(where, velocity.reshape(DZ * DY, NX), *([sums] if r == 0 else []))


def regroup(arrays, tiles, with_sums):
    def kernel(*refs):
        for i in range(4):
            for k in range(4):
                refs[4 + i][k * tiles : (k + 1) * tiles] = refs[k][i * tiles : (i + 1) * tiles]
            if with_sums:
                last = 4 * tiles
                refs[4 + i][last] = (refs[0][last] + refs[1][last]) + (refs[2][last] + refs[3][last])

    shape = jax.ShapeDtypeStruct((4 * tiles + (1 if with_sums else 0), 8, BX), F32)
    return pl.pallas_call(
        kernel,
        in_specs=[VM] * 4,
        out_specs=[VM] * 4,
        out_shape=[shape] * 4,
        compiler_params=params(),
        name="regroup",
    )(*arrays)


def shift(value, axis, by):
    moves = []
    for i in range(N):
        x, y = i // 4, i % 4
        moves.append((i, ((x + by) % 4) * 4 + y if axis == "x" else x * 4 + (y + by) % 4))
    return lax.ppermute(value, "pz", moves)


def send_stage(arrays, axis, sign):
    return [arrays[0]] + [shift(arrays[k], axis, sign * k) for k in range(1, 4)]


def z_kernel(where_ref, after_ref, high_hbm, low_hbm, *refs):
    ins_hbm, outs_hbm, refs = refs[:8], refs[8:16], refs[16:]
    ins, outs, (high_ref, low_ref, lines_ref, sems) = refs[:8], refs[8:16], refs[16:]
    move = Mover(sems)
    fetch = [move.start(ins_hbm[i], ins[i]) for i in range(8)]
    fetch_matrix = [move.start(high_hbm, high_ref), move.start(low_hbm, low_ref)]
    away = []

    def spots(r, k2):
        route = ROUTES[r]
        first, second = places(route, where_ref)
        tiles, width = tiles_of(route), len(route[2])
        for k1 in range(4):
            device = device_at(route, (first - k1) % 4, (second - k2) % 4)
            for rt in range(3):
                at = k1 * tiles + rt * width
                into = rt * 9 + route[2][0]
                yield device, slice(at, at + width), slice(into, into + width)

    for r in range(2):
        for k2 in range(4):
            fetch[r * 4 + k2].wait()
            for device, outer, inner in spots(r, k2):
                lines_ref[device, inner] = ins[r * 4 + k2][outer]
    wait(fetch_matrix)
    for r, columns in enumerate((ROUTES[0][2], ROUTES[1][2])):
        tiles = []
        for j in columns:
            tiles.append(jnp.stack([lines_ref[:, rt * 9 + j] for rt in range(3)], axis=1).reshape(N * 24, BX))
        high, low = halves(jnp.concatenate(tiles, axis=1))
        got = dot(high_ref[...], high) + dot(low_ref[...], high) + dot(high_ref[...], low)
        for k, j in enumerate(columns):
            value = got[:, k * BX : k * BX + BX].reshape(N, 3, 8, BX)
            for rt in range(3):
                lines_ref[:, rt * 9 + j] = value[:, rt]
        for k2 in range(4):
            for device, outer, inner in spots(r, k2):
                outs[r * 4 + k2][outer] = lines_ref[device, inner]
            away.append(move.start(outs[r * 4 + k2], outs_hbm[r * 4 + k2]))
    wait(away)


def z_lines(where, after, arrays):
    high, low = z_matrix()
    shapes = []
    for r, route in enumerate(ROUTES):
        shapes += [jax.ShapeDtypeStruct((4 * tiles_of(route), 8, BX), F32)] * 4
    return pl.pallas_call(
        z_kernel,
        in_specs=[SM, VM] + [HB] * 10,
        out_specs=[HB] * 8,
        out_shape=shapes,
        scratch_shapes=[pltpu.VMEM(a.shape, F32) for a in arrays]
        + [pltpu.VMEM(a.shape, F32) for a in shapes]
        + [
            pltpu.VMEM((N * 24, N * 24), BF16),
            pltpu.VMEM((N * 24, N * 24), BF16),
            pltpu.VMEM((N, 27, 8, BX), F32),
            pltpu.SemaphoreType.DMA((18,)),
        ],
        compiler_params=params(WHOLE),
        name="z_lines",
    )(where, after, jnp.asarray(high), jnp.asarray(low), *arrays)


def z_unpack_kernel(where_ref, term_ref, *refs):
    out_ref, sum_ref = refs[8:]
    for r, route in enumerate(ROUTES):
        first, second = places(route, where_ref)
        width = len(route[2])
        for k1 in range(4):
            got = refs[r * 4 + k1]
            for k2 in range(4):
                device = device_at(route, (first + k1) % 4, (second + k2) % 4)
                for n, j in enumerate(route[2]):
                    y, low_cols = columns_of(device, j, 0)
                    y, high_cols = columns_of(device, j, 1)
                    base = k2 * 3 * width + n
                    for at, count, cols, tile, row in (
                        (0, 8, low_cols, base, 0),
                        (8, 4, low_cols, base + width, 0),
                        (0, 4, high_cols, base + width, 4),
                        (4, 8, high_cols, base + 2 * width, 0),
                    ):
                        spot = pl.ds(y + at * DY, count, stride=DY)
                        sum_ref[cols, spot, :] = got[tile, row : row + count]

    for xb in range(XB):
        cols = slice(xb * BX, xb * BX + BX)
        out_ref[:, cols] = term_ref[:, cols] + sum_ref[xb]


def z_unpack(where, term, arrays):
    return pl.pallas_call(
        z_unpack_kernel,
        in_specs=[SM] + [VM] * 9,
        out_specs=VM,
        out_shape=jax.ShapeDtypeStruct((DZ * DY, NX), F32),
        scratch_shapes=[pltpu.VMEM((XB, DZ * DY, BX), F32)],
        compiler_params=params(),
        name="z_unpack",
    )(where, term.reshape(DZ * DY, NX), *arrays).reshape(DZ, DY, NX)


def sigmoid(value):
    return 1.0 / (1.0 + jnp.exp(-value))


def axial(rel):
    return jnp.exp(-0.5 * (rel / DISK_DEPTH) ** 2)


def radial(rel_z, rel_y):
    return sigmoid((RADIUS * RADIUS - rel_y * rel_y - rel_z * rel_z) / (2.0 * RADIUS))


def disk_kernel(where_ref, wind_ref, brick_ref, offset_ref, v_ref, sums_ref, high_ref, low_ref, radial_ref, hold_ref, ahead_ref, behind_ref):
    level, column = where_ref[0], where_ref[3]
    sums_ref[...] = jnp.zeros((8, BX), F32)

    @pl.when(level < 2)
    def _():
        hold_ref[...] = jnp.zeros((8, BX), F32)
        hold_ref[0:1, 0:TURB] = brick_ref[0:1, :].astype(F32)
        hold_ref[1:4, 0:TURB] = offset_ref[...].astype(F32)
        brick, centre_z, centre_y, centre_x = (hold_ref[i : i + 1, :] for i in range(4))
        line = jnp.floor((brick + 0.5) * (1.0 / XB))
        block = brick - XB * line
        left = line - N * jnp.floor((line + 0.5) * (1.0 / N))
        shifted = column.astype(F32) - left
        lane = lax.broadcasted_iota(jnp.int32, (1, BX), 1)
        here = ((shifted == 0.0) | (shifted == 1.0)) & (lane < TURB)
        block = jnp.where(here, block, -1.0)
        sub = lax.broadcasted_iota(jnp.int32, (8, BX), 0).astype(F32)
        along = lax.broadcasted_iota(jnp.int32, (BX, BX), 0).astype(F32)
        shape_x = axial(along - centre_x)
        depth = jnp.sum(shape_x, axis=0, keepdims=True)
        for xb in range(XB):
            weight = jnp.where(block == float(xb), shape_x, 0.0)
            high, low = halves(weight)
            ahead_ref[xb * BX : xb * BX + BX] = high
            behind_ref[xb * BX : xb * BX + BX] = low
            high, low = halves(weight.T)
            high_ref[:, xb * BX : xb * BX + BX] = high
            low_ref[:, xb * BX : xb * BX + BX] = low
        high, low = halves(v_ref[...].reshape(DZ * DY, NX))
        along_disk = dot(high, ahead_ref[...]) + dot(low, ahead_ref[...]) + dot(high, behind_ref[...])
        base_z = (level * DZ).astype(F32) - centre_z
        base_y = shifted * float(DY) - centre_y
        total = jnp.zeros((8, BX), F32)
        for z in range(DZ):
            for yt in range(3):
                rows = slice(z * DY + yt * 8, z * DY + yt * 8 + 8)
                weight = jnp.where(here, radial(base_z + float(z), sub + (base_y + 8.0 * yt)), 0.0)
                radial_ref[rows] = weight
                total = total + weight * (along_disk[rows] + wind_ref[z] * depth)
        sums_ref[0:1] = jnp.sum(total, axis=0, keepdims=True)


def disks(where, wind, bricks, offset, velocity):
    return pl.pallas_call(
        disk_kernel,
        in_specs=[SM, SM, VM, VM, VM],
        out_specs=[VM] * 4,
        out_shape=[
            jax.ShapeDtypeStruct((8, BX), F32),
            jax.ShapeDtypeStruct((BX, NX), BF16),
            jax.ShapeDtypeStruct((BX, NX), BF16),
            jax.ShapeDtypeStruct((DZ * DY, BX), F32),
        ],
        scratch_shapes=[
            pltpu.VMEM((8, BX), F32),
            pltpu.VMEM((NX, BX), BF16),
            pltpu.VMEM((NX, BX), BF16),
        ],
        compiler_params=params(16),
        name="disks",
    )(where, wind, bricks.T, offset.T, velocity)


def final_kernel(where_ref, coef_ref, denom_ref, high_ref, low_ref, radial_ref, terms_ref, lines_ref, out_ref, speed_ref, held_ref, push_ref, sem):
    level = where_ref[0]
    total = lines_ref[0, 27]
    for d in range(1, N):
        total = total + lines_ref[d, 27]
    speed = total[0:1, :] / denom_ref[0:1, :]
    speed_ref[...] = speed[:, :TURB]

    def emit(force):
        copies = []
        for part in range(4):
            for local in range(36 * part, 36 * part + 36):
                z, xb = local // XB, local % XB
                cols = slice(xb * BX, xb * BX + BX)
                for yt in range(3):
                    rows = slice(yt * 8, yt * 8 + 8)
                    value = terms_ref[z, rows, cols] + lines_ref[local // 9, yt * 9 + local % 9]
                    if force is not None:
                        value = value + force[z * DY + yt * 8 : z * DY + yt * 8 + 8, cols]
                    held_ref[z, rows, cols] = value
            span = pl.ds(3 * part, 3)
            copies.append(pltpu.make_async_copy(held_ref.at[span], out_ref.at[span], sem.at[part]))
            copies[-1].start()
        for copy in copies:
            copy.wait()

    @pl.when(level < 2)
    def _():
        push_ref[...] = jnp.zeros((8, BX), F32)
        push_ref[0:1, :TURB] = -0.5 * coef_ref[...] * speed[:, :TURB] * jnp.abs(speed[:, :TURB])
        high, low = halves(radial_ref[...] * push_ref[0:1, :])
        emit(dot(high, high_ref[...]) + dot(low, high_ref[...]) + dot(high, low_ref[...]))

    @pl.when(level >= 2)
    def _():
        emit(None)


def finish(where, coef, denom, basis, terms, lines):
    tendency, speed = pl.pallas_call(
        final_kernel,
        in_specs=[SM] + [VM] * 7,
        out_specs=[HB, VM],
        out_shape=[jax.ShapeDtypeStruct((DZ, DY, NX), F32), jax.ShapeDtypeStruct((1, TURB), F32)],
        scratch_shapes=[
            pltpu.VMEM((DZ, DY, NX), F32),
            pltpu.VMEM((8, BX), F32),
            pltpu.SemaphoreType.DMA((4,)),
        ],
        compiler_params=params(16),
        name="finish",
    )(where, coef, denom, *basis, terms, lines)
    return tendency, speed.reshape(TURB)


def body(velocity, wind, thrust_coef, bricks, offset):
    pz, py = lax.axis_index("pz"), lax.axis_index("py")
    packed = y_pack(velocity)
    packed, pz, py = lax.optimization_barrier((packed, pz, py))
    where = jnp.stack([pz, pz // 4, pz % 4, py]).astype(jnp.int32)
    with jax.named_scope("spanwise_send"):
        received = lax.all_to_all(packed, "py", 0, 0, tiled=True)
    sums, *basis = disks(where, wind, bricks, offset, velocity)
    with jax.named_scope("vertical_send"):
        arrived = []
        for r, route in enumerate(ROUTES):
            stage = send_stage(z_pack(r, where, velocity, sums), route[0], 1)
            stage = regroup(stage, tiles_of(route), r == 0)
            arrived += send_stage(stage, route[1], 1)
    term_x, denom = along_x(velocity, wind, offset)
    spanwise, after = y_lines(level_sums(arrived), received)
    vertical = z_lines(where, after, arrived)
    with jax.named_scope("spanwise_return"):
        returned = lax.all_to_all(spanwise, "py", 0, 0, tiled=True)
    with jax.named_scope("vertical_return"):
        back = []
        for r, route in enumerate(ROUTES):
            stage = send_stage(vertical[4 * r : 4 * r + 4], route[1], -1)
            stage = regroup(stage, tiles_of(route), False)
            back += send_stage(stage, route[0], -1)
    terms = z_unpack(where, term_x, back)
    return finish(where, thrust_coef.reshape(1, TURB), denom, basis, terms, returned)


def solution(mesh):
    return jax.shard_map(
        body,
        mesh=mesh,
        in_specs=(P("pz", "py", None), P("pz"), P(), P(), P()),
        out_specs=(P("pz", "py", None), P()),
        check_vma=False,
    )
```
